512 devices in a mesh: dp: 16 (over z_lo, core), tensor: 4 (over y), expert: 8 (over x, z_hi).
Axes of the slice: x: 4, y: 4, z: 16 (z_hi: 2, z_lo: 8; z = z_hi * 8 + z_lo), core: 2. Of those that a mesh axis runs over, the one named last changes fastest.
Arguments:
- latent: bfloat16 [131072, 384], P(('dp', 'expert')), may hold values from -20 to 20
- out_grad: bfloat16 [131072, 64, 128], P(('dp', 'expert'), 'tensor'), may hold values from -20000 to 20000
- lengths: int32 [2, 256], P(None, ('dp', 'expert')), may hold values from 85 to 512, as said below
- momentum: float32 [128, 384, 64], P(('dp', 'expert'), None, 'tensor'), may hold values from -1.5 to 1.5
- accumulated: float32 [128, 384, 64], P(('dp', 'expert'), None, 'tensor'), may hold values from -1.5 to 1.5
Outputs:
- update: float32 [128, 384, 64], P(('dp', 'expert'), None, 'tensor')
- momentum_new: float32 [128, 384, 64], P(('dp', 'expert'), None, 'tensor')
The draws below stay inside these ranges and needn't reach their ends.
Inputs may be any that keep to these rules, and one draw needn't show every extreme that they name: `lengths`: slots at or past a sequence's length are padding.
All inputs are finite; a program needn't handle non-finite values.
Results may differ from the reference program's by a relative error of at most 0.035.
Values may be sent and summed in bfloat16 or wider, within the bound.
A program may use at most 64 MiB of HBM per device.

```python
import math
import jax
import jax.numpy as jnp
from jax import lax

KVR = 384
HD = 64
SEQ_LEN = 512
SEQ_DEV = 2
MB = 2
ITERS = 5
TOK_DEV = 1024
NSEQ = 256
TOKENS = 131072
MATS = 128


def scales_from(key, count, highest):
    return jnp.exp(jax.random.uniform(key, count, jnp.float32, 0.0, math.log(highest)))


def draw_latent(key, part):
    key = jax.random.fold_in(key, 11)
    first_key, second_key = jax.random.split(key)
    base = jnp.clip(jax.random.normal(first_key, (TOKENS, KVR), jnp.float32), -6.0, 6.0)
    scales = scales_from(second_key, (KVR,), 3.16)
    return (base * scales[None, :]).astype(jnp.bfloat16)


def draw_out_grad(key, part):
    key = jax.random.fold_in(key, 23)
    first_key, second_key, third_key = jax.random.split(key, 3)
    base = jnp.clip(jax.random.normal(first_key, (TOKENS, HD, MATS), jnp.float32), -6.0, 6.0)
    scales = scales_from(second_key, (HD, MATS), 3.16)
    pairing = jax.random.permutation(third_key, MATS)
    block_index = jnp.arange(TOKENS, dtype=jnp.int32) // TOK_DEV
    paired = pairing[block_index]
    spike = jnp.where(paired[:, None, None] == jnp.arange(MATS, dtype=jnp.int32)[None, None, :], 8.0, 1.0)
    return (128.0 * base * scales[None, :, :] * spike).astype(jnp.bfloat16)


def draw_lengths(key, part):
    key = jax.random.fold_in(key, 37)
    devices = NSEQ // SEQ_DEV
    lowest_cap = SEQ_LEN // 3
    seq_index = jnp.arange(NSEQ, dtype=jnp.int32)
    device_index = seq_index // SEQ_DEV
    ceiling = lowest_cap + (SEQ_LEN - lowest_cap) * device_index // max(devices - 1, 1)
    shortfall = jax.random.randint(key, (MB, NSEQ), 0, ceiling[None, :] // 2 + 1, dtype=jnp.int32)
    lengths_out = ceiling[None, :] - shortfall
    micro_index = jnp.arange(MB, dtype=jnp.int32)[:, None]
    lengths_out = jnp.where((micro_index == MB - 1) & (seq_index[None, :] == NSEQ - 1), SEQ_LEN, lengths_out)
    lengths_out = jnp.where((micro_index == 0) & (seq_index[None, :] == 0), lowest_cap - lowest_cap // 2, lengths_out)
    return lengths_out.astype(jnp.int32)


def levels(own_key, shape, cuts, low, top_value):
    def one(dim, blocks):
        steps = jax.random.uniform(jax.random.fold_in(jax.random.fold_in(own_key, 6), dim), (blocks,), jnp.float32, low / len(cuts), top_value / len(cuts))
        return jnp.repeat(jnp.exp(steps), shape[dim] // blocks).reshape((-1,) + (1,) * (len(shape) - dim - 1))

    factor_of = one(*cuts[0])
    for cut in cuts[1:]:
        factor_of = factor_of * one(*cut)
    return factor_of


def bell_draw(key, extent, deviation, most, pieces=(), kind=jnp.bfloat16):
    result = jax.random.normal(key, extent, jnp.float32) * deviation
    if len(pieces) > 0:
        result = levels(key, extent, pieces, -0.22, 0.18) * result
    return jnp.clip(result, min=-most, max=most).astype(kind)


def setup_inputs(seed: int = 0) -> dict:
    seeds = jax.random.split(jax.random.key(seed), 6)
    return {
        "latent": draw_latent(jax.random.fold_in(seeds[5], 71), 0),
        "out_grad": draw_out_grad(jax.random.fold_in(seeds[5], 71), 0),
        "lengths": draw_lengths(jax.random.fold_in(seeds[5], 71), 0),
        "momentum": bell_draw(seeds[3], (MATS, KVR, HD), (max(1, TOKENS // 8192)) ** -0.5, 1.5, ((0, 128), (2, 4)), jnp.float32),
        "accumulated": bell_draw(seeds[4], (MATS, KVR, HD), (max(1, TOKENS // 8192)) ** -0.5, 1.5, ((0, 128), (2, 4)), jnp.float32),
    }


EPSILON = 1e-07
COEFF_A = 3.4445
COEFF_B = -4.775
COEFF_C = 2.0315
DECAY = 0.95

def reference(latent, out_grad, lengths, momentum, accumulated):
    limits = lengths[MB - 1]
    keep_rows = (jnp.arange(SEQ_LEN, dtype=jnp.int32)[None, :] < limits[:, None]).reshape(TOKENS)
    masked = jnp.where(keep_rows[:, None], latent, jnp.zeros_like(latent))
    blocks = TOKENS // TOK_DEV
    left = masked.reshape(blocks, TOK_DEV, KVR)
    right = out_grad.reshape(blocks, TOK_DEV, HD * MATS)

    def accumulate(carry, pair):
        product = jnp.dot(pair[0].astype(jnp.float32).T, pair[1].astype(jnp.float32), precision=lax.Precision.HIGHEST)
        return (carry + product, None)
    summed, unused = lax.scan(accumulate, jnp.zeros((KVR, HD * MATS), jnp.float32), (left, right))
    grad = jnp.transpose(summed.reshape(KVR, HD, MATS), (2, 0, 1))
    token_total = jnp.sum(lengths, dtype=jnp.int32).astype(jnp.float32)
    combined = DECAY * momentum + accumulated + grad / token_total
    norms = jnp.sqrt(lax.optimization_barrier(jnp.sum(combined * combined, axis=(1, 2))))
    iterate = (combined / (norms + EPSILON)[:, None, None]).astype(jnp.bfloat16)
    for iteration in range(ITERS):
        current = iterate.astype(jnp.float32)
        gram = jnp.einsum('mrc,mrd->mcd', current, current, precision=lax.Precision.HIGHEST)
        squared = jnp.einsum('mcd,mde->mce', gram, gram, precision=lax.Precision.HIGHEST)
        poly = (COEFF_B * gram + COEFF_C * squared).astype(jnp.bfloat16)
        moved = jnp.einsum('mrc,mce->mre', current, poly.astype(jnp.float32), precision=lax.Precision.HIGHEST)
        iterate = (COEFF_A * current + moved).astype(jnp.bfloat16)
    factor = 0.2 * math.sqrt(max(KVR, HD))
    update = factor * iterate.astype(jnp.float32)
    return (update, combined)
```

```python
import functools
import math

import jax
import jax.numpy as jnp
from jax import lax
from jax.experimental import pallas as pl
from jax.experimental.pallas import tpu as pltpu
from jax.sharding import PartitionSpec as P

ITERS = 5
EPSILON = 1e-07
COEFF_A = 3.4445
COEFF_B = -4.775
COEFF_C = 2.0315
DECAY = 0.95

TOK = 1024
KVR = 384
COLS = 16
MATS = 128
NX = 4
NY = 4
NZ = 16
SEQ = 512
CHUNKS = 4
NC = COLS // CHUNKS
LOADS = 4
F32 = jnp.float32
BF16 = jnp.bfloat16
MESH = pl.DeviceIdType.MESH


def device(core, x, y, z):
    return (lax.rem(z, 8) * 2 + core, y, x * 2 + z // 8)


def orthogonalize(iterate):
    for _ in range(ITERS):
        gram = lax.dot_general(
            iterate, iterate, (((1,), (1,)), ((), ())), preferred_element_type=F32
        )
        squared = jnp.dot(gram, gram, precision=lax.Precision.HIGHEST)
        poly = (COEFF_B * gram + COEFF_C * squared).astype(BF16)
        moved = jnp.dot(poly, iterate, preferred_element_type=F32)
        iterate = (COEFF_A * iterate.astype(F32) + moved).astype(BF16)
    return iterate


def kernel(
    lat_hbm, og_hbm, len_hbm, mom_hbm, acc_hbm, upd_ref, new_ref,
    lat, og, lens, mom, acc, flat, lat_t, right, turned,
    send_a, recv_a, send_x, recv_x, part, send_z, recv_z, gathered, last,
    cnt_a, cnt_x, cnt_z,
    lat_sem, og_sem, len_sem, mom_sem,
    a_ss, a_rs, x_ss, x_rs, z_ss, z_rs, y_ss, y_rs,
    ca_ss, ca_rs, cx_ss, cx_rs, cz_ss, cz_rs,
):
    dp = lax.axis_index("dp")
    y = lax.axis_index("tensor")
    expert = lax.axis_index("expert")
    core = lax.rem(dp, 2)
    x = expert // 2
    z = lax.rem(expert, 2) * 8 + dp // 2

    sibling = device(1 - core, x, y, z)
    x_peers = [device(core, lax.rem(x + d, NX), y, z) for d in range(1, NX)]
    y_peers = [device(core, x, lax.rem(y + d, NY), z) for d in range(1, NY)]
    z_order = sorted(range(1, NZ), key=lambda d: -min(d, NZ - d))
    z_peers = {d: device(core, x, y, lax.rem(z + d, NZ)) for d in z_order}

    barrier = pltpu.get_barrier_semaphore()
    for peer in [z_peers[d] for d in z_order] + x_peers + y_peers + [sibling]:
        pl.semaphore_signal(barrier, inc=1, device_id=peer, device_id_type=MESH)

    step = TOK // LOADS
    len_copy = pltpu.make_async_copy(len_hbm, lens, len_sem)
    len_copy.start()
    lat_copy = pltpu.make_async_copy(lat_hbm, lat, lat_sem)
    lat_copy.start()
    og_copies = []
    for i in range(LOADS):
        cut = pl.ds(i * step, step)
        copy = pltpu.make_async_copy(og_hbm.at[cut], og.at[cut], og_sem.at[i])
        copy.start()
        og_copies.append(copy)
    mom_copies = [
        pltpu.make_async_copy(mom_hbm, mom, mom_sem.at[0]),
        pltpu.make_async_copy(acc_hbm, acc, mom_sem.at[1]),
    ]
    for copy in mom_copies:
        copy.start()

    len_copy.wait()
    own = lens[0, 0] + lens[0, 1] + lens[1, 0] + lens[1, 1]
    cnt_a[0] = jnp.full((8, 128), own, jnp.int32)

    lat_copy.wait()
    token = lax.broadcasted_iota(jnp.int32, (TOK, 1), 0)
    limit = jnp.where(token < SEQ, lens[1, 0], lens[1, 1] + SEQ)
    masked = jnp.where(token < limit, lat[...].astype(F32), 0.0)
    lat_t[...] = masked.T.astype(BF16)

    for i in range(LOADS):
        og_copies[i].wait()

        def regroup(j, _):
            base = pl.multiple_of(i * step + j * 32, 32)
            for h in range(2):
                rows = og[pl.ds(base + h * 16, 16)].astype(F32)
                flat[h] = rows.reshape(16 * COLS, MATS)
                for c in range(COLS):
                    picked = flat[h, pl.ds(c, 16, stride=COLS), :]
                    right[c // 2, pl.ds(base + h * 16, 16), (c % 2) * MATS : (c % 2 + 1) * MATS] = (
                        picked.astype(BF16)
                    )
            return 0

        lax.fori_loop(0, step // 32, regroup, 0)

    pl.semaphore_wait(barrier, 1 + (NX - 1) + (NY - 1) + (NZ - 1))

    def count_copy(src, dst, ss, rs, peer):
        return pltpu.make_async_remote_copy(src, dst, ss, rs, device_id=peer, device_id_type=MESH)

    ca = count_copy(cnt_a.at[0], cnt_a.at[1], ca_ss, ca_rs, sibling)
    ca.start()

    def multiply(k):
        for p in range(k * NC // 2, (k + 1) * NC // 2):
            product = jnp.dot(lat_t[...], right[p], preferred_element_type=F32)
            for h in range(2):
                c = p * 2 + h
                for b in range(KVR // 128):
                    lanes = slice(b * 128, (b + 1) * 128)
                    turned[h, b] = product[lanes, h * MATS : (h + 1) * MATS].T
                    for cc in range(2):
                        for xx in range(NX):
                            q = cc * 8 + xx * 2
                            low = turned[h, b, pl.ds(q, 8, stride=16), :]
                            high = turned[h, b, pl.ds(q + 1, 8, stride=16), :]
                            send_a[k, cc, xx, c - k * NC, :, lanes] = jnp.concatenate(
                                [low, high], 0
                            ).astype(BF16)

    def core_copy(k):
        return pltpu.make_async_remote_copy(
            send_a.at[k, 1 - core], recv_a.at[k], a_ss.at[k], a_rs.at[k],
            device_id=sibling, device_id_type=MESH,
        )

    def pair_sum(k, xx):
        return send_a[k, core, xx].astype(F32) + recv_a[k, xx].astype(F32)

    def x_copy(k, d):
        return pltpu.make_async_remote_copy(
            send_x.at[k, d - 1], recv_x.at[k, d - 1], x_ss.at[k, d - 1], x_rs.at[k, d - 1],
            device_id=x_peers[d - 1], device_id_type=MESH,
        )

    def z_copy(k, d):
        return pltpu.make_async_remote_copy(
            send_z.at[k, lax.rem(z + d, NZ)], recv_z.at[k, d - 1], z_ss.at[k, d - 1], z_rs.at[k, d - 1],
            device_id=z_peers[d], device_id_type=MESH,
        )

    cx = [count_copy(cnt_x.at[0], cnt_x.at[d], cx_ss.at[d - 1], cx_rs.at[d - 1], x_peers[d - 1]) for d in range(1, NX)]
    cz = [count_copy(cnt_z.at[0], cnt_z.at[d], cz_ss.at[d - 1], cz_rs.at[d - 1], z_peers[d]) for d in range(1, NZ)]

    def start_x(k):
        core_copy(k).wait_recv()
        if k == 0:
            ca.wait_recv()
            cnt_x[0] = cnt_a[0] + cnt_a[1]
            for copy in cx:
                copy.start()
        for d in (2, 1, 3):
            send_x[k, d - 1] = pair_sum(k, lax.rem(x + d, NX)).astype(BF16)
            x_copy(k, d).start()

    def start_z(k):
        if k == 0:
            for copy in cx:
                copy.wait_recv()
            cnt_z[0] = cnt_x[0] + cnt_x[1] + cnt_x[2] + cnt_x[3]
            for copy in cz:
                copy.start()
        total = pair_sum(k, x)
        for d in (1, 3, 2):
            x_copy(k, d).wait_recv()
            total = total + recv_x[k, d - 1].astype(F32)
        total = total.reshape(NC * NZ, KVR)
        for b in range(KVR // 128):
            lanes = slice(b * 128, (b + 1) * 128)
            part[b] = total[:, lanes]
            for t in range(NZ):
                send_z[k, t, :, lanes] = part[b, pl.ds(t, NC, stride=NZ), :].astype(BF16)
        for d in z_order:
            z_copy(k, d).start()

    for k in range(CHUNKS):
        multiply(k)
        core_copy(k).start()
        if k >= 1:
            start_x(k - 1)
        if k >= 3:
            start_z(k - 3)
    start_x(CHUNKS - 1)
    for k in range(max(0, CHUNKS - 3), CHUNKS):
        start_z(k)

    for copy in mom_copies:
        copy.wait()
    count = cnt_z[0]
    for d in range(1, NZ):
        cz[d - 1].wait_recv()
        count = count + cnt_z[d]
    scale = 1.0 / count[0:1, 0:1].astype(F32)
    for k in range(CHUNKS):
        grad = send_z[k, z].astype(F32)
        for d in reversed(z_order):
            z_copy(k, d).wait_recv()
            grad = grad + recv_z[k, d - 1].astype(F32)
        cut = pl.ds(k * NC, NC)
        gathered[y, cut] = DECAY * mom[cut] + acc[cut] + grad * scale

    y_copies = [
        pltpu.make_async_remote_copy(
            gathered.at[y], gathered.at[y], y_ss.at[d - 1], y_rs.at[d - 1],
            device_id=y_peers[d - 1], device_id_type=MESH,
        )
        for d in range(1, NY)
    ]
    y_waits = [
        pltpu.make_async_remote_copy(
            gathered.at[lax.rem(y + NY - d, NY)], gathered.at[lax.rem(y + NY - d, NY)],
            y_ss.at[d - 1], y_rs.at[d - 1], device_id=y_peers[d - 1], device_id_type=MESH,
        )
        for d in range(1, NY)
    ]
    for d in (2, 1, 3):
        y_copies[d - 1].start()
    new_ref[...] = gathered[y]
    ca.wait_send()
    for k in range(CHUNKS):
        core_copy(k).wait_send()
        for d in range(1, NX):
            x_copy(k, d).wait_send()
        for d in range(1, NZ):
            z_copy(k, d).wait_send()
    for copy in cx + cz:
        copy.wait_send()
    for copy in y_waits:
        copy.wait_recv()
    full = gathered[...].reshape(NY * COLS, KVR)
    norm = jnp.sqrt(jnp.sum(full * full, axis=(0, 1), keepdims=True))
    iterate = orthogonalize((full / (norm + EPSILON)).astype(BF16))
    factor = 0.2 * math.sqrt(max(KVR, NY * COLS))
    last[...] = (factor * iterate.astype(F32)).reshape(NY, COLS, KVR)
    upd_ref[...] = last[y]
    for copy in y_copies:
        copy.wait_send()


def fused(latent, out_grad, lengths, momentum, accumulated):
    any_spec = pl.BlockSpec(memory_space=pl.ANY)
    vmem_spec = pl.BlockSpec(memory_space=pltpu.VMEM)
    block = jax.ShapeDtypeStruct((COLS, KVR), F32)
    dma = pltpu.SemaphoreType.DMA
    return pl.pallas_call(
        kernel,
        out_shape=(block, block),
        in_specs=[any_spec] * 5,
        out_specs=(vmem_spec, vmem_spec),
        scratch_shapes=[
            pltpu.VMEM((TOK, KVR), BF16),
            pltpu.VMEM((TOK, COLS, MATS), BF16),
            pltpu.SMEM((2, 2), jnp.int32),
            pltpu.VMEM((COLS, KVR), F32),
            pltpu.VMEM((COLS, KVR), F32),
            pltpu.VMEM((2, 16 * COLS, MATS), F32),
            pltpu.VMEM((KVR, TOK), BF16),
            pltpu.VMEM((COLS // 2, TOK, 2 * MATS), BF16),
            pltpu.VMEM((2, KVR // 128, MATS, 128), F32),
            pltpu.VMEM((CHUNKS, 2, NX, NC, NZ, KVR), BF16),
            pltpu.VMEM((CHUNKS, NX, NC, NZ, KVR), BF16),
            pltpu.VMEM((CHUNKS, NX - 1, NC, NZ, KVR), BF16),
            pltpu.VMEM((CHUNKS, NX - 1, NC, NZ, KVR), BF16),
            pltpu.VMEM((KVR // 128, NC * NZ, 128), F32),
            pltpu.VMEM((CHUNKS, NZ, NC, KVR), BF16),
            pltpu.VMEM((CHUNKS, NZ - 1, NC, KVR), BF16),
            pltpu.VMEM((NY, COLS, KVR), F32),
            pltpu.VMEM((NY, COLS, KVR), F32),
            pltpu.VMEM((2, 8, 128), jnp.int32),
            pltpu.VMEM((NX, 8, 128), jnp.int32),
            pltpu.VMEM((NZ, 8, 128), jnp.int32),
            dma, dma((LOADS,)), dma, dma((2,)),
            dma((CHUNKS,)), dma((CHUNKS,)),
            dma((CHUNKS, NX - 1)), dma((CHUNKS, NX - 1)),
            dma((CHUNKS, NZ - 1)), dma((CHUNKS, NZ - 1)),
            dma((NY - 1,)), dma((NY - 1,)),
            dma, dma, dma((NX - 1,)), dma((NX - 1,)), dma((NZ - 1,)), dma((NZ - 1,)),
        ],
        compiler_params=pltpu.CompilerParams(
            collective_id=0, has_side_effects=True, vmem_limit_bytes=48 << 20
        ),
        name="muon_step",
    )(latent, out_grad, lengths, momentum, accumulated)


def per_device(latent, out_grad, lengths, momentum, accumulated):
    update, combined = fused(
        latent,
        out_grad,
        lengths,
        jnp.swapaxes(momentum[0], 0, 1),
        jnp.swapaxes(accumulated[0], 0, 1),
    )
    return (jnp.swapaxes(update, 0, 1)[None], jnp.swapaxes(combined, 0, 1)[None])


def solution(mesh):
    owned = P(("dp", "expert"), None, "tensor")
    in_specs = (
        P(("dp", "expert"), None),
        P(("dp", "expert"), "tensor", None),
        P(None, ("dp", "expert")),
        owned,
        owned,
    )
    return jax.shard_map(
        per_device, mesh=mesh, in_specs=in_specs, out_specs=(owned, owned), check_vma=False
    )
```

```python
import functools
import math

import jax
import jax.numpy as jnp
from jax import lax
from jax.experimental import pallas as pl
from jax.experimental.pallas import tpu as pltpu
from jax.sharding import PartitionSpec as P

ITERS = 5
EPSILON = 1e-07
COEFF_A = 3.4445
COEFF_B = -4.775
COEFF_C = 2.0315
DECAY = 0.95

TOK = 1024
KVR = 384
COLS = 16
MATS = 128
NX = 4
NY = 4
NZ = 16
SEQ = 512
CHUNKS = 4
NC = COLS // CHUNKS
LOADS = 4
PITCH = 17
F32 = jnp.float32
BF16 = jnp.bfloat16
MESH = pl.DeviceIdType.MESH


def device(core, x, y, z):
    return (lax.rem(z, 8) * 2 + core, y, x * 2 + z // 8)


def orthogonalize(iterate):
    for _ in range(ITERS):
        gram = lax.dot_general(
            iterate, iterate, (((1,), (1,)), ((), ())), preferred_element_type=F32
        )
        squared = jnp.dot(gram, gram, precision=lax.Precision.HIGHEST)
        poly = (COEFF_B * gram + COEFF_C * squared).astype(BF16)
        moved = jnp.dot(poly, iterate, preferred_element_type=F32)
        iterate = (COEFF_A * iterate.astype(F32) + moved).astype(BF16)
    return iterate


def kernel(
    lat_hbm, og_hbm, len_hbm, mom_hbm, acc_hbm, upd_ref, new_ref,
    lat, og, lens, mom, acc, flat, lat_t, right, turned,
    send_a, recv_a, send_x, recv_x, part, send_z, recv_z, gathered, last,
    cnt_a, cnt_x, cnt_z,
    known, lat_sem, og_sem, len_sem, mom_sem,
    a_ss, a_rs, x_ss, x_rs, z_ss, z_rs, y_ss, y_rs,
    ca_ss, ca_rs, cx_ss, cx_rs, cz_ss, cz_rs,
):
    dp = lax.axis_index("dp")
    y = lax.axis_index("tensor")
    expert = lax.axis_index("expert")
    core = lax.rem(dp, 2)
    x = expert // 2
    z = lax.rem(expert, 2) * 8 + dp // 2

    sibling = device(1 - core, x, y, z)
    x_peers = [device(core, lax.rem(x + d, NX), y, z) for d in range(1, NX)]
    y_peers = [device(core, x, lax.rem(y + d, NY), z) for d in range(1, NY)]
    z_order = sorted(range(1, NZ), key=lambda d: -min(d, NZ - d))
    z_peers = {d: device(core, x, y, lax.rem(z + d, NZ)) for d in z_order}

    barrier = pltpu.get_barrier_semaphore()
    near = [x_peers[1], y_peers[1], z_peers[2], z_peers[NZ - 2], x_peers[0], x_peers[2]]
    near += [y_peers[0], y_peers[2], z_peers[1], z_peers[NZ - 1], sibling]
    for peer in near:
        pl.semaphore_signal(barrier, inc=1, device_id=peer, device_id_type=MESH)

    step = TOK // LOADS
    len_copy = pltpu.make_async_copy(len_hbm, lens, len_sem)
    len_copy.start()
    lat_copy = pltpu.make_async_copy(lat_hbm, lat, lat_sem)
    lat_copy.start()
    og_copies = []
    for i in range(LOADS):
        cut = pl.ds(i * step, step)
        copy = pltpu.make_async_copy(og_hbm.at[cut], og.at[cut], og_sem.at[i])
        copy.start()
        og_copies.append(copy)
    mom_copies = [
        pltpu.make_async_copy(mom_hbm, mom, mom_sem.at[0]),
        pltpu.make_async_copy(acc_hbm, acc, mom_sem.at[1]),
    ]
    for copy in mom_copies:
        copy.start()

    len_copy.wait()
    own = lens[0, 0] + lens[0, 1] + lens[1, 0] + lens[1, 1]
    cnt_a[0] = jnp.full((8, 128), own, jnp.int32)

    lat_copy.wait()
    token = lax.broadcasted_iota(jnp.int32, (TOK, 1), 0)
    limit = jnp.where(token < SEQ, lens[1, 0], lens[1, 1] + SEQ)
    masked = jnp.where(token < limit, lat[...].astype(F32), 0.0)
    lat_t[...] = masked.T.astype(BF16)

    for i in range(LOADS):
        og_copies[i].wait()

        def regroup(j, _):
            base = pl.multiple_of(i * step + j * 32, 32)
            for h in range(2):
                rows = og[pl.ds(base + h * 16, 16)].astype(F32)
                for t in range(16):
                    flat[h, pl.ds(t, COLS, stride=PITCH), :] = rows[t]
                for c in range(COLS):
                    picked = flat[h, pl.ds(c * PITCH, 16), :]
                    right[c // 2, pl.ds(base + h * 16, 16), (c % 2) * MATS : (c % 2 + 1) * MATS] = (
                        picked.astype(BF16)
                    )
            return 0

        lax.fori_loop(0, step // 32, regroup, 0)
        if i == LOADS // 2 - 1:
            pl.semaphore_wait(barrier, len(near))
            for d in (2, NZ - 2):
                pl.semaphore_signal(known.at[0], inc=1, device_id=z_peers[d], device_id_type=MESH)

    def multiply(k):
        for p in range(k * NC // 2, (k + 1) * NC // 2):
            product = jnp.dot(lat_t[...], right[p], preferred_element_type=F32)
            for h in range(2):
                c = p * 2 + h
                for b in range(KVR // 128):
                    lanes = slice(b * 128, (b + 1) * 128)
                    block = product[lanes, h * MATS : (h + 1) * MATS].T
                    for t in range(8):
                        turned[h, b, pl.ds(t * PITCH, 16), :] = block[t * 16 : (t + 1) * 16]
                    for cc in range(2):
                        for xx in range(NX):
                            q = cc * 8 + xx * 2
                            low = turned[h, b, pl.ds(q, 8, stride=PITCH), :]
                            high = turned[h, b, pl.ds(q + 1, 8, stride=PITCH), :]
                            send_a[k, cc, xx, c - k * NC, :, lanes] = jnp.concatenate(
                                [low, high], 0
                            ).astype(BF16)

    multiply(0)

    def count_copy(src, dst, ss, rs, peer):
        return pltpu.make_async_remote_copy(src, dst, ss, rs, device_id=peer, device_id_type=MESH)

    ca = count_copy(cnt_a.at[0], cnt_a.at[1], ca_ss, ca_rs, sibling)
    ca.start()

    def core_copy(k):
        return pltpu.make_async_remote_copy(
            send_a.at[k, 1 - core], recv_a.at[k], a_ss.at[k], a_rs.at[k],
            device_id=sibling, device_id_type=MESH,
        )

    def pair_sum(k, xx):
        return send_a[k, core, xx].astype(F32) + recv_a[k, xx].astype(F32)

    def x_copy(k, d):
        return pltpu.make_async_remote_copy(
            send_x.at[k, d - 1], recv_x.at[k, d - 1], x_ss.at[k, d - 1], x_rs.at[k, d - 1],
            device_id=x_peers[d - 1], device_id_type=MESH,
        )

    def z_copy(k, d):
        return pltpu.make_async_remote_copy(
            send_z.at[k, lax.rem(z + d, NZ)], recv_z.at[k, d - 1], z_ss.at[k, d - 1], z_rs.at[k, d - 1],
            device_id=z_peers[d], device_id_type=MESH,
        )

    cx = [count_copy(cnt_x.at[0], cnt_x.at[d], cx_ss.at[d - 1], cx_rs.at[d - 1], x_peers[d - 1]) for d in range(1, NX)]
    cz = [count_copy(cnt_z.at[0], cnt_z.at[d], cz_ss.at[d - 1], cz_rs.at[d - 1], z_peers[d]) for d in range(1, NZ)]

    def start_x(k):
        core_copy(k).wait_recv()
        if k == 0:
            ca.wait_recv()
            cnt_x[0] = cnt_a[0] + cnt_a[1]
            for copy in cx:
                copy.start()
        for d in (2, 1, 3):
            send_x[k, d - 1] = pair_sum(k, lax.rem(x + d, NX)).astype(BF16)
            x_copy(k, d).start()

    def start_z(k):
        if k == 0:
            for copy in cx:
                copy.wait_recv()
            cnt_z[0] = cnt_x[0] + cnt_x[1] + cnt_x[2] + cnt_x[3]
            for copy in cz:
                copy.start()
        total = pair_sum(k, x)
        for d in (1, 3, 2):
            x_copy(k, d).wait_recv()
            total = total + recv_x[k, d - 1].astype(F32)
        for b in range(KVR // 128):
            lanes = slice(b * 128, (b + 1) * 128)
            for c in range(NC):
                part[b, pl.ds(c * PITCH, NZ), :] = total[c, :, lanes]
            for t in range(NZ):
                send_z[k, t, :, lanes] = part[b, pl.ds(t, NC, stride=PITCH), :].astype(BF16)
        for d in z_order:
            z_copy(k, d).start()

    for k in range(CHUNKS):
        if k >= 1:
            multiply(k)
        core_copy(k).start()
        if k == 1:
            pl.semaphore_wait(known.at[0], 2)
            for d in (4, NZ - 4):
                pl.semaphore_signal(known.at[1], inc=1, device_id=z_peers[d], device_id_type=MESH)
        if k >= 1:
            start_x(k - 1)
    start_x(CHUNKS - 1)
    pl.semaphore_wait(known.at[1], 2)
    for k in range(CHUNKS):
        start_z(k)

    for copy in mom_copies:
        copy.wait()
    count = cnt_z[0]
    for d in range(1, NZ):
        cz[d - 1].wait_recv()
        count = count + cnt_z[d]
    scale = 1.0 / count[0:1, 0:1].astype(F32)
    for k in range(CHUNKS):
        grad = send_z[k, z].astype(F32)
        for d in reversed(z_order):
            z_copy(k, d).wait_recv()
            grad = grad + recv_z[k, d - 1].astype(F32)
        cut = pl.ds(k * NC, NC)
        gathered[y, cut] = DECAY * mom[cut] + acc[cut] + grad * scale

    y_copies = [
        pltpu.make_async_remote_copy(
            gathered.at[y], gathered.at[y], y_ss.at[d - 1], y_rs.at[d - 1],
            device_id=y_peers[d - 1], device_id_type=MESH,
        )
        for d in range(1, NY)
    ]
    y_waits = [
        pltpu.make_async_remote_copy(
            gathered.at[lax.rem(y + NY - d, NY)], gathered.at[lax.rem(y + NY - d, NY)],
            y_ss.at[d - 1], y_rs.at[d - 1], device_id=y_peers[d - 1], device_id_type=MESH,
        )
        for d in range(1, NY)
    ]
    for d in (2, 1, 3):
        y_copies[d - 1].start()
    new_ref[...] = gathered[y]
    ca.wait_send()
    for k in range(CHUNKS):
        core_copy(k).wait_send()
        for d in range(1, NX):
            x_copy(k, d).wait_send()
        for d in range(1, NZ):
            z_copy(k, d).wait_send()
    for copy in cx + cz:
        copy.wait_send()
    for copy in y_waits:
        copy.wait_recv()
    full = gathered[...].reshape(NY * COLS, KVR)
    norm = jnp.sqrt(jnp.sum(full * full, axis=(0, 1), keepdims=True))
    iterate = orthogonalize((full / (norm + EPSILON)).astype(BF16))
    factor = 0.2 * math.sqrt(max(KVR, NY * COLS))
    last[...] = (factor * iterate.astype(F32)).reshape(NY, COLS, KVR)
    upd_ref[...] = last[y]
    for copy in y_copies:
        copy.wait_send()


def fused(*operands):
    hbm_spec = pl.BlockSpec(memory_space=pltpu.HBM)
    vmem_spec = pl.BlockSpec(memory_space=pltpu.VMEM)
    block = jax.ShapeDtypeStruct((COLS, KVR), F32)
    dma = pltpu.SemaphoreType.DMA
    return pl.pallas_call(
        kernel,
        out_shape=(block, block),
        in_specs=[hbm_spec] * 5,
        out_specs=(vmem_spec, vmem_spec),
        scratch_shapes=[
            pltpu.VMEM((TOK, KVR), BF16),
            pltpu.VMEM((TOK, COLS, MATS), BF16),
            pltpu.SMEM((2, 2), jnp.int32),
            pltpu.VMEM((COLS, KVR), F32),
            pltpu.VMEM((COLS, KVR), F32),
            pltpu.VMEM((2, COLS * PITCH, MATS), F32),
            pltpu.VMEM((KVR, TOK), BF16),
            pltpu.VMEM((COLS // 2, TOK, 2 * MATS), BF16),
            pltpu.VMEM((2, KVR // 128, 8 * PITCH, 128), F32),
            pltpu.VMEM((CHUNKS, 2, NX, NC, NZ, KVR), BF16),
            pltpu.VMEM((CHUNKS, NX, NC, NZ, KVR), BF16),
            pltpu.VMEM((CHUNKS, NX - 1, NC, NZ, KVR), BF16),
            pltpu.VMEM((CHUNKS, NX - 1, NC, NZ, KVR), BF16),
            pltpu.VMEM((KVR // 128, NC * PITCH, 128), F32),
            pltpu.VMEM((CHUNKS, NZ, NC, KVR), BF16),
            pltpu.VMEM((CHUNKS, NZ - 1, NC, KVR), BF16),
            pltpu.VMEM((NY, COLS, KVR), F32),
            pltpu.VMEM((NY, COLS, KVR), F32),
            pltpu.VMEM((2, 8, 128), jnp.int32),
            pltpu.VMEM((NX, 8, 128), jnp.int32),
            pltpu.VMEM((NZ, 8, 128), jnp.int32),
            pltpu.SemaphoreType.REGULAR((2,)),
            dma, dma((LOADS,)), dma, dma((2,)),
            dma((CHUNKS,)), dma((CHUNKS,)),
            dma((CHUNKS, NX - 1)), dma((CHUNKS, NX - 1)),
            dma((CHUNKS, NZ - 1)), dma((CHUNKS, NZ - 1)),
            dma((NY - 1,)), dma((NY - 1,)),
            dma, dma, dma((NX - 1,)), dma((NX - 1,)), dma((NZ - 1,)), dma((NZ - 1,)),
        ],
        compiler_params=pltpu.CompilerParams(
            collective_id=0, has_side_effects=True, vmem_limit_bytes=48 << 20
        ),
        name="muon_step",
    )(*[pltpu.with_memory_space_constraint(v, pltpu.HBM) for v in operands])


def per_device(latent, out_grad, lengths, momentum, accumulated):
    update, combined = fused(
        latent,
        out_grad,
        lengths,
        jnp.swapaxes(momentum[0], 0, 1),
        jnp.swapaxes(accumulated[0], 0, 1),
    )
    return (jnp.swapaxes(update, 0, 1)[None], jnp.swapaxes(combined, 0, 1)[None])


def solution(mesh):
    owned = P(("dp", "expert"), None, "tensor")
    in_specs = (
        P(("dp", "expert"), None),
        P(("dp", "expert"), "tensor", None),
        P(None, ("dp", "expert")),
        owned,
        owned,
    )
    return jax.shard_map(
        per_device, mesh=mesh, in_specs=in_specs, out_specs=(owned, owned), check_vma=False
    )
```

```python
import functools
import math

import jax
import jax.numpy as jnp
from jax import lax
from jax.experimental import pallas as pl
from jax.experimental.pallas import tpu as pltpu
from jax.sharding import PartitionSpec as P

ITERS = 5
EPSILON = 1e-07
COEFF_A = 3.4445
COEFF_B = -4.775
COEFF_C = 2.0315
DECAY = 0.95

TOK = 1024
KVR = 384
COLS = 16
MATS = 128
NX = 4
NY = 4
NZ = 16
SEQ = 512
CHUNKS = 4
NC = COLS // CHUNKS
LOADS = 4
PITCH = 17
F32 = jnp.float32
BF16 = jnp.bfloat16
MESH = pl.DeviceIdType.MESH


def device(core, x, y, z):
    return (lax.rem(z, 8) * 2 + core, y, x * 2 + z // 8)


def orthogonalize(iterate):
    for _ in range(ITERS):
        gram = lax.dot_general(
            iterate, iterate, (((1,), (1,)), ((), ())), preferred_element_type=F32
        )
        high = gram.astype(BF16)
        low = (gram - high.astype(F32)).astype(BF16)
        squared = (
            jnp.dot(high, high, preferred_element_type=F32)
            + jnp.dot(high, low, preferred_element_type=F32)
            + jnp.dot(low, high, preferred_element_type=F32)
        )
        poly = (COEFF_B * gram + COEFF_C * squared).astype(BF16)
        moved = jnp.dot(poly, iterate, preferred_element_type=F32)
        iterate = (COEFF_A * iterate.astype(F32) + moved).astype(BF16)
    return iterate


def kernel(
    lat_hbm, og_hbm, len_hbm, mom_hbm, acc_hbm, all_ref,
    lat, og, lens, mom, acc, flat, lat_t, right, turned,
    send_a, recv_a, send_x, recv_x, part, send_z, recv_z, gathered,
    cnt_a, cnt_x, cnt_z,
    known, lat_sem, og_sem, len_sem, mom_sem,
    a_ss, a_rs, x_ss, x_rs, z_ss, z_rs, y_ss, y_rs,
    ca_ss, ca_rs, cx_ss, cx_rs, cz_ss, cz_rs,
):
    dp = lax.axis_index("dp")
    y = lax.axis_index("tensor")
    expert = lax.axis_index("expert")
    core = lax.rem(dp, 2)
    x = expert // 2
    z = lax.rem(expert, 2) * 8 + dp // 2

    sibling = device(1 - core, x, y, z)
    x_peers = [device(core, lax.rem(x + d, NX), y, z) for d in range(1, NX)]
    y_peers = [device(core, x, lax.rem(y + d, NY), z) for d in range(1, NY)]
    z_order = sorted(range(1, NZ), key=lambda d: -min(d, NZ - d))
    z_peers = {d: device(core, x, y, lax.rem(z + d, NZ)) for d in z_order}

    barrier = pltpu.get_barrier_semaphore()
    near = [z_peers[d] for d in (4, NZ - 4, 3, NZ - 3)]
    near += [x_peers[1], y_peers[1], z_peers[2], z_peers[NZ - 2], x_peers[0], x_peers[2]]
    near += [y_peers[0], y_peers[2], z_peers[1], z_peers[NZ - 1], sibling]
    for peer in near:
        pl.semaphore_signal(barrier, inc=1, device_id=peer, device_id_type=MESH)

    step = TOK // LOADS
    len_copy = pltpu.make_async_copy(len_hbm, lens, len_sem)
    len_copy.start()
    lat_copy = pltpu.make_async_copy(lat_hbm, lat, lat_sem)
    lat_copy.start()
    og_copies = []
    for i in range(LOADS):
        cut = pl.ds(i * step, step)
        copy = pltpu.make_async_copy(og_hbm.at[cut], og.at[cut], og_sem.at[i])
        copy.start()
        og_copies.append(copy)
    mom_copies = [
        pltpu.make_async_copy(mom_hbm, mom, mom_sem.at[0]),
        pltpu.make_async_copy(acc_hbm, acc, mom_sem.at[1]),
    ]
    for copy in mom_copies:
        copy.start()

    len_copy.wait()
    own = lens[0, 0] + lens[0, 1] + lens[1, 0] + lens[1, 1]
    cnt_a[0] = jnp.full((8, 128), own, jnp.int32)

    lat_copy.wait()
    token = lax.broadcasted_iota(jnp.int32, (TOK, 1), 0)
    limit = jnp.where(token < SEQ, lens[1, 0], lens[1, 1] + SEQ)
    masked = jnp.where(token < limit, lat[...].astype(F32), 0.0)
    lat_t[...] = masked.T.astype(BF16)

    for i in range(LOADS):
        og_copies[i].wait()

        def regroup(j, _):
            base = pl.multiple_of(i * step + j * 32, 32)
            for h in range(2):
                rows = og[pl.ds(base + h * 16, 16)].astype(F32)
                for t in range(16):
                    flat[h, pl.ds(t, COLS, stride=PITCH), :] = rows[t]
                for c in range(COLS):
                    picked = flat[h, pl.ds(c * PITCH, 16), :]
                    right[c // 2, pl.ds(base + h * 16, 16), (c % 2) * MATS : (c % 2 + 1) * MATS] = (
                        picked.astype(BF16)
                    )
            return 0

        lax.fori_loop(0, step // 32, regroup, 0)

    def multiply(k):
        for p in range(k * NC // 2, (k + 1) * NC // 2):
            product = jnp.dot(lat_t[...], right[p], preferred_element_type=F32)
            for h in range(2):
                c = p * 2 + h
                for b in range(KVR // 128):
                    lanes = slice(b * 128, (b + 1) * 128)
                    block = product[lanes, h * MATS : (h + 1) * MATS].T
                    for t in range(8):
                        turned[h, b, pl.ds(t * PITCH, 16), :] = block[t * 16 : (t + 1) * 16]
                    for cc in range(2):
                        for xx in range(NX):
                            q = cc * 8 + xx * 2
                            low = turned[h, b, pl.ds(q, 8, stride=PITCH), :]
                            high = turned[h, b, pl.ds(q + 1, 8, stride=PITCH), :]
                            send_a[k, cc, xx, c - k * NC, :, lanes] = jnp.concatenate(
                                [low, high], 0
                            ).astype(BF16)

    multiply(0)
    pl.semaphore_wait(barrier, len(near))
    for d in (4, NZ - 4):
        pl.semaphore_signal(known, inc=1, device_id=z_peers[d], device_id_type=MESH)

    def count_copy(src, dst, ss, rs, peer):
        return pltpu.make_async_remote_copy(src, dst, ss, rs, device_id=peer, device_id_type=MESH)

    ca = count_copy(cnt_a.at[0], cnt_a.at[1], ca_ss, ca_rs, sibling)

    def core_copy(k):
        return pltpu.make_async_remote_copy(
            send_a.at[k, 1 - core], recv_a.at[k], a_ss.at[k], a_rs.at[k],
            device_id=sibling, device_id_type=MESH,
        )

    def pair_sum(k, xx):
        return send_a[k, core, xx].astype(F32) + recv_a[k, xx].astype(F32)

    def x_copy(k, d):
        return pltpu.make_async_remote_copy(
            send_x.at[k, d - 1], recv_x.at[k, d - 1], x_ss.at[k], x_rs.at[k],
            device_id=x_peers[d - 1], device_id_type=MESH,
        )

    def z_copy(k, d):
        return pltpu.make_async_remote_copy(
            send_z.at[k, lax.rem(z + d, NZ)], recv_z.at[k, d - 1], z_ss.at[k], z_rs.at[k],
            device_id=z_peers[d], device_id_type=MESH,
        )

    def settle(ref, sem):
        pltpu.make_async_copy(ref, ref, sem).wait()

    cx = [
        count_copy(cnt_x.at[0], cnt_x.at[d], cx_ss, cx_rs, x_peers[d - 1]) for d in range(1, NX)
    ]
    cz = [
        count_copy(cnt_z.at[0, 0], cnt_z.at[0, 1 + n], cz_ss.at[0], cz_rs.at[0], z_peers[d])
        for n, d in enumerate((1, NZ - 1, 2))
    ]
    cw = [
        count_copy(cnt_z.at[1, 0], cnt_z.at[1, 1 + n], cz_ss.at[1], cz_rs.at[1], z_peers[d])
        for n, d in enumerate((4, NZ - 4, 8))
    ]

    def total_of(ref, sem):
        settle(ref.at[pl.ds(1, 3)], sem)
        return ref[0] + ref[1] + ref[2] + ref[3]

    def start_count(k):
        if k == 0:
            cnt_z[0, 0] = total_of(cnt_x, cx_rs)
            for copy in cz:
                copy.start()
        if k == 1:
            cnt_z[1, 0] = total_of(cnt_z.at[0], cz_rs.at[0])
            for copy in cw:
                copy.start()

    def start_x(k):
        core_copy(k).wait_recv()
        for d in (2, 1, 3):
            send_x[k, d - 1] = pair_sum(k, lax.rem(x + d, NX)).astype(BF16)
            x_copy(k, d).start()
        if k == 0:
            ca.wait_recv()
            cnt_x[0] = cnt_a[0] + cnt_a[1]
            for copy in cx:
                copy.start()

    def start_z(k):
        total = pair_sum(k, x)
        settle(recv_x.at[k], x_rs.at[k])
        for d in (1, 3, 2):
            total = total + recv_x[k, d - 1].astype(F32)
        for b in range(KVR // 128):
            for c in range(NC):
                part[b, pl.ds(c * PITCH, NZ), :] = total[c, :, b * 128 : (b + 1) * 128]
        for d in z_order + [0]:
            t = lax.rem(z + d, NZ)
            for b in range(KVR // 128):
                send_z[k, t, :, b * 128 : (b + 1) * 128] = part[b, pl.ds(t, NC, stride=PITCH), :].astype(BF16)
            if d:
                z_copy(k, d).start()

    for k in range(CHUNKS):
        if k >= 1:
            multiply(k)
        core_copy(k).start()
        if k == 0:
            ca.start()
        if k >= 1:
            start_x(k - 1)
    start_x(CHUNKS - 1)
    pl.semaphore_wait(known, 2)
    for k in range(CHUNKS):
        start_z(k)
        start_count(k)

    for copy in mom_copies:
        copy.wait()
    count = total_of(cnt_z.at[1], cz_rs.at[1])
    scale = 1.0 / count[0:1, 0:1].astype(F32)

    def y_copy(half, d):
        return pltpu.make_async_remote_copy(
            gathered.at[y, half], gathered.at[y, half], y_ss, y_rs.at[d - 1],
            device_id=y_peers[d - 1], device_id_type=MESH,
        )

    for k in range(CHUNKS):
        grad = send_z[k, z].astype(F32)
        settle(recv_z.at[k], z_rs.at[k])
        for d in z_order:
            grad = grad + recv_z[k, d - 1].astype(F32)
        half, cut = k * NC // 8, pl.ds(k * NC % 8, NC)
        own = pl.ds(k * NC, NC)
        gathered[y, half, cut] = DECAY * mom[own] + acc[own] + grad * scale
        if (k + 1) * NC % 8 == 0:
            for d in (2, 1, 3):
                y_copy(half, d).start()
    ca.wait_send()
    for k in range(CHUNKS):
        core_copy(k).wait_send()
        settle(recv_x.at[k], x_ss.at[k])
        settle(recv_z.at[k], z_ss.at[k])
    settle(cnt_x.at[pl.ds(1, NX - 1)], cx_ss)
    for n in range(2):
        settle(cnt_z.at[n, pl.ds(1, 3)], cz_ss.at[n])
    for d in range(1, NY):
        settle(gathered.at[lax.rem(y + NY - d, NY)], y_rs.at[d - 1])
    all_ref[...] = gathered[...].reshape(NY, COLS, KVR)
    for d in range(1, NY):
        settle(gathered.at[y], y_ss)


def finish(all_ref, upd_hbm, new_hbm, last, sem):
    y = lax.axis_index("tensor")
    keep = pltpu.make_async_copy(all_ref.at[y], new_hbm, sem.at[0])
    keep.start()
    full = all_ref[...].reshape(NY * COLS, KVR)
    norm = jnp.sqrt(jnp.sum(full * full, axis=(0, 1), keepdims=True))
    iterate = orthogonalize((full / (norm + EPSILON)).astype(BF16))
    factor = 0.2 * math.sqrt(max(KVR, NY * COLS))
    last[...] = (factor * iterate.astype(F32)).reshape(NY, COLS, KVR)
    out = pltpu.make_async_copy(last.at[y], upd_hbm, sem.at[1])
    out.start()
    keep.wait()
    out.wait()


def fused(*operands):
    hbm_spec = pl.BlockSpec(memory_space=pltpu.HBM)
    vmem_spec = pl.BlockSpec(memory_space=pltpu.VMEM)
    any_spec = pl.BlockSpec(memory_space=pl.ANY)
    block = jax.ShapeDtypeStruct((COLS, KVR), F32)
    dma = pltpu.SemaphoreType.DMA
    gathered = pl.pallas_call(
        kernel,
        out_shape=jax.ShapeDtypeStruct((NY, COLS, KVR), F32),
        in_specs=[hbm_spec] * 5,
        out_specs=vmem_spec,
        scratch_shapes=[
            pltpu.VMEM((TOK, KVR), BF16),
            pltpu.VMEM((TOK, COLS, MATS), BF16),
            pltpu.SMEM((2, 2), jnp.int32),
            pltpu.VMEM((COLS, KVR), F32),
            pltpu.VMEM((COLS, KVR), F32),
            pltpu.VMEM((2, COLS * PITCH, MATS), F32),
            pltpu.VMEM((KVR, TOK), BF16),
            pltpu.VMEM((COLS // 2, TOK, 2 * MATS), BF16),
            pltpu.VMEM((2, KVR // 128, 8 * PITCH, 128), F32),
            pltpu.VMEM((CHUNKS, 2, NX, NC, NZ, KVR), BF16),
            pltpu.VMEM((CHUNKS, NX, NC, NZ, KVR), BF16),
            pltpu.VMEM((CHUNKS, NX - 1, NC, NZ, KVR), BF16),
            pltpu.VMEM((CHUNKS, NX - 1, NC, NZ, KVR), BF16),
            pltpu.VMEM((KVR // 128, NC * PITCH, 128), F32),
            pltpu.VMEM((CHUNKS, NZ, NC, KVR), BF16),
            pltpu.VMEM((CHUNKS, NZ - 1, NC, KVR), BF16),
            pltpu.VMEM((NY, 2, COLS // 2, KVR), F32),
            pltpu.VMEM((2, 8, 128), jnp.int32),
            pltpu.VMEM((NX, 8, 128), jnp.int32),
            pltpu.VMEM((2, 4, 8, 128), jnp.int32),
            pltpu.SemaphoreType.REGULAR,
            dma, dma((LOADS,)), dma, dma((2,)),
            dma((CHUNKS,)), dma((CHUNKS,)),
            dma((CHUNKS,)), dma((CHUNKS,)), dma((CHUNKS,)), dma((CHUNKS,)),
            dma, dma((NY - 1,)),
            dma, dma, dma, dma, dma((2,)), dma((2,)),
        ],
        compiler_params=pltpu.CompilerParams(
            collective_id=0, has_side_effects=True, vmem_limit_bytes=48 << 20
        ),
        name="muon_step",
    )(*[pltpu.with_memory_space_constraint(v, pltpu.HBM) for v in operands])
    return pl.pallas_call(
        finish,
        out_shape=(block, block),
        in_specs=[vmem_spec],
        out_specs=(any_spec, any_spec),
        scratch_shapes=[pltpu.VMEM((NY, COLS, KVR), F32), dma((2,))],
        compiler_params=pltpu.CompilerParams(vmem_limit_bytes=8 << 20),
        name="orthogonal_update",
    )(gathered)


def per_device(latent, out_grad, lengths, momentum, accumulated):
    update, combined = fused(
        latent,
        out_grad,
        lengths,
        jnp.swapaxes(momentum[0], 0, 1),
        jnp.swapaxes(accumulated[0], 0, 1),
    )
    return (jnp.swapaxes(update, 0, 1)[None], jnp.swapaxes(combined, 0, 1)[None])


def solution(mesh):
    owned = P(("dp", "expert"), None, "tensor")
    in_specs = (
        P(("dp", "expert"), None),
        P(("dp", "expert"), "tensor", None),
        P(None, ("dp", "expert")),
        owned,
        owned,
    )
    return jax.shard_map(
        per_device, mesh=mesh, in_specs=in_specs, out_specs=(owned, owned), check_vma=False
    )
```

```python
import functools
import math

import jax
import jax.numpy as jnp
from jax import lax
from jax.experimental import pallas as pl
from jax.experimental.pallas import tpu as pltpu
from jax.sharding import PartitionSpec as P

ITERS = 5
EPSILON = 1e-07
COEFF_A = 3.4445
COEFF_B = -4.775
COEFF_C = 2.0315
DECAY = 0.95

TOK = 1024
KVR = 384
COLS = 16
MATS = 128
NX = 4
NY = 4
NZ = 16
SEQ = 512
CHUNKS = 4
NC = COLS // CHUNKS
LOADS = 4
PITCH = 17
F32 = jnp.float32
BF16 = jnp.bfloat16
MESH = pl.DeviceIdType.MESH


def device(core, x, y, z):
    return (lax.rem(z, 8) * 2 + core, y, x * 2 + z // 8)


def orthogonalize(iterate):
    wide = iterate.astype(F32)
    scale = 1.0 / (jnp.sqrt(jnp.sum(wide * wide, axis=(0, 1), keepdims=True)) + EPSILON)
    for step in range(ITERS):
        gram = lax.dot_general(
            iterate, iterate, (((1,), (1,)), ((), ())), preferred_element_type=F32
        )
        if step == 0:
            gram = gram * scale * scale
        high = gram.astype(BF16)
        low = (gram - high.astype(F32)).astype(BF16)
        squared = (
            jnp.dot(high, high, preferred_element_type=F32)
            + jnp.dot(high, low, preferred_element_type=F32)
            + jnp.dot(low, high, preferred_element_type=F32)
        )
        poly = (COEFF_B * gram + COEFF_C * squared).astype(BF16)
        moved = COEFF_A * iterate.astype(F32) + jnp.dot(poly, iterate, preferred_element_type=F32)
        if step == 0:
            moved = moved * scale
        iterate = moved.astype(BF16)
    return iterate


def kernel(
    lat_hbm, og_hbm, len_hbm, mom_hbm, acc_hbm, all_ref, new_ref,
    lat, og, lens, mom, acc, flat, lat_t, right, turned,
    send_a, recv_a, send_x, recv_x, part, send_z, recv_z, gathered,
    cnt_a, cnt_x, cnt_z,
    known, lat_sem, og_sem, len_sem, mom_sem,
    a_ss, a_rs, x_ss, x_rs, z_ss, z_rs, y_ss, y_rs,
    ca_ss, ca_rs, cx_ss, cx_rs, cz_ss, cz_rs,
):
    dp = lax.axis_index("dp")
    y = lax.axis_index("tensor")
    expert = lax.axis_index("expert")
    core = lax.rem(dp, 2)
    x = expert // 2
    z = lax.rem(expert, 2) * 8 + dp // 2

    sibling = device(1 - core, x, y, z)
    x_peers = [device(core, lax.rem(x + d, NX), y, z) for d in range(1, NX)]
    y_peers = [device(core, x, lax.rem(y + d, NY), z) for d in range(1, NY)]
    z_order = sorted(range(1, NZ), key=lambda d: -min(d, NZ - d))
    z_peers = {d: device(core, x, y, lax.rem(z + d, NZ)) for d in z_order}

    step = TOK // LOADS
    len_copy = pltpu.make_async_copy(len_hbm, lens, len_sem)
    len_copy.start()
    lat_copy = pltpu.make_async_copy(lat_hbm, lat, lat_sem)
    lat_copy.start()
    og_copies = []
    for i in range(LOADS):
        cut = pl.ds(i * step, step)
        copy = pltpu.make_async_copy(og_hbm.at[cut], og.at[cut], og_sem.at[i])
        copy.start()
        og_copies.append(copy)
    barrier = pltpu.get_barrier_semaphore()
    near = [z_peers[d] for d in (4, NZ - 4, 3, NZ - 3)]
    near += [x_peers[1], y_peers[1], z_peers[2], z_peers[NZ - 2], x_peers[0], x_peers[2]]
    near += [y_peers[0], y_peers[2], z_peers[1], z_peers[NZ - 1], sibling]
    for peer in near:
        pl.semaphore_signal(barrier, inc=1, device_id=peer, device_id_type=MESH)

    mom_copies = [
        pltpu.make_async_copy(mom_hbm, mom, mom_sem.at[0]),
        pltpu.make_async_copy(acc_hbm, acc, mom_sem.at[1]),
    ]
    for copy in mom_copies:
        copy.start()

    len_copy.wait()
    own = lens[0, 0] + lens[0, 1] + lens[1, 0] + lens[1, 1]
    cnt_a[0] = jnp.full((8, 128), own, jnp.int32)

    lat_copy.wait()
    token = lax.broadcasted_iota(jnp.int32, (TOK, 1), 0)
    limit = jnp.where(token < SEQ, lens[1, 0], lens[1, 1] + SEQ)
    masked = jnp.where(token < limit, lat[...].astype(F32), 0.0)
    lat_t[...] = masked.T.astype(BF16)

    for i in range(LOADS):
        og_copies[i].wait()

        def regroup(j, _):
            base = pl.multiple_of(i * step + j * 32, 32)
            for h in range(2):
                rows = og[pl.ds(base + h * 16, 16)].astype(F32)
                for t in range(16):
                    flat[h, pl.ds(t, COLS, stride=PITCH), :] = rows[t]
                for c in range(COLS):
                    picked = flat[h, pl.ds(c * PITCH, 16), :]
                    right[c // 2, pl.ds(base + h * 16, 16), (c % 2) * MATS : (c % 2 + 1) * MATS] = (
                        picked.astype(BF16)
                    )
            return 0

        lax.fori_loop(0, step // 32, regroup, 0)

    def multiply(k):
        for p in range(k * NC // 2, (k + 1) * NC // 2):
            product = jnp.dot(lat_t[...], right[p], preferred_element_type=F32)
            for h in range(2):
                c = p * 2 + h
                for b in range(KVR // 128):
                    lanes = slice(b * 128, (b + 1) * 128)
                    block = product[lanes, h * MATS : (h + 1) * MATS].T
                    for t in range(8):
                        turned[h, b, pl.ds(t * PITCH, 16), :] = block[t * 16 : (t + 1) * 16]
                    for cc in range(2):
                        for xx in range(NX):
                            q = cc * 8 + xx * 2
                            low = turned[h, b, pl.ds(q, 8, stride=PITCH), :]
                            high = turned[h, b, pl.ds(q + 1, 8, stride=PITCH), :]
                            send_a[k, cc, xx, c - k * NC, :, lanes] = jnp.concatenate(
                                [low, high], 0
                            ).astype(BF16)

    pl.semaphore_wait(barrier, len(near))
    for d in (4, NZ - 4):
        pl.semaphore_signal(known, inc=1, device_id=z_peers[d], device_id_type=MESH)
    multiply(0)

    def count_copy(src, dst, ss, rs, peer):
        return pltpu.make_async_remote_copy(src, dst, ss, rs, device_id=peer, device_id_type=MESH)

    ca = count_copy(cnt_a.at[0], cnt_a.at[1], ca_ss, ca_rs, sibling)

    def core_copy(k):
        return pltpu.make_async_remote_copy(
            send_a.at[k, 1 - core], recv_a.at[k], a_ss.at[k], a_rs.at[k],
            device_id=sibling, device_id_type=MESH,
        )

    def pair_sum(k, xx):
        return send_a[k, core, xx].astype(F32) + recv_a[k, xx].astype(F32)

    def x_copy(k, d):
        return pltpu.make_async_remote_copy(
            send_x.at[k, d - 1], recv_x.at[k, d - 1], x_ss.at[k], x_rs.at[k],
            device_id=x_peers[d - 1], device_id_type=MESH,
        )

    def z_copy(k, d):
        return pltpu.make_async_remote_copy(
            send_z.at[k, lax.rem(z + d, NZ)], recv_z.at[k, d - 1], z_ss.at[k], z_rs.at[k],
            device_id=z_peers[d], device_id_type=MESH,
        )

    def settle(ref, sem):
        pltpu.make_async_copy(ref, ref, sem).wait()

    cx = [
        count_copy(cnt_x.at[0], cnt_x.at[d], cx_ss, cx_rs, x_peers[d - 1]) for d in range(1, NX)
    ]
    cz = [
        count_copy(cnt_z.at[0, 0], cnt_z.at[0, 1 + n], cz_ss.at[0], cz_rs.at[0], z_peers[d])
        for n, d in enumerate((1, NZ - 1, 2))
    ]
    cw = [
        count_copy(cnt_z.at[1, 0], cnt_z.at[1, 1 + n], cz_ss.at[1], cz_rs.at[1], z_peers[d])
        for n, d in enumerate((4, NZ - 4, 8))
    ]

    def total_of(ref, sem):
        settle(ref.at[pl.ds(1, 3)], sem)
        return ref[0] + ref[1] + ref[2] + ref[3]

    def start_count(k):
        if k == 0:
            cnt_z[0, 0] = total_of(cnt_x, cx_rs)
            for copy in cz:
                copy.start()
        if k == 1:
            cnt_z[1, 0] = total_of(cnt_z.at[0], cz_rs.at[0])
            for copy in cw:
                copy.start()

    def start_x(k):
        core_copy(k).wait_recv()
        for d in (2, 1, 3):
            send_x[k, d - 1] = pair_sum(k, lax.rem(x + d, NX)).astype(BF16)
            x_copy(k, d).start()
        if k == 0:
            ca.wait_recv()
            cnt_x[0] = cnt_a[0] + cnt_a[1]
            for copy in cx:
                copy.start()

    def start_z(k):
        total = pair_sum(k, x)
        settle(recv_x.at[k], x_rs.at[k])
        for d in (1, 3, 2):
            total = total + recv_x[k, d - 1].astype(F32)
        for b in range(KVR // 128):
            for c in range(NC):
                part[b, pl.ds(c * PITCH, NZ), :] = total[c, :, b * 128 : (b + 1) * 128]
        for d in z_order + [0]:
            t = lax.rem(z + d, NZ)
            for b in range(KVR // 128):
                send_z[k, t, :, b * 128 : (b + 1) * 128] = part[b, pl.ds(t, NC, stride=PITCH), :].astype(BF16)
            if d:
                z_copy(k, d).start()

    for k in range(CHUNKS):
        if k >= 1:
            multiply(k)
        core_copy(k).start()
        if k == 0:
            ca.start()
        if k >= 1:
            start_x(k - 1)
    start_x(CHUNKS - 1)
    pl.semaphore_wait(known, 2)
    for k in range(CHUNKS):
        start_z(k)
        start_count(k)

    for copy in mom_copies:
        copy.wait()
    count = total_of(cnt_z.at[1], cz_rs.at[1])
    scale = 1.0 / count[0:1, 0:1].astype(F32)

    for k in range(CHUNKS):
        grad = send_z[k, z].astype(F32)
        settle(recv_z.at[k], z_rs.at[k])
        for d in z_order:
            grad = grad + recv_z[k, d - 1].astype(F32)
        own = pl.ds(k * NC, NC)
        new_ref[own] = DECAY * mom[own] + acc[own] + grad * scale
    gathered[y] = new_ref[...].astype(BF16)

    def y_copy(d):
        return pltpu.make_async_remote_copy(
            gathered.at[y], gathered.at[y], y_ss, y_rs.at[d - 1],
            device_id=y_peers[d - 1], device_id_type=MESH,
        )

    for d in (2, 1, 3):
        y_copy(d).start()
    ca.wait_send()
    for k in range(CHUNKS):
        core_copy(k).wait_send()
        settle(recv_x.at[k], x_ss.at[k])
        settle(recv_z.at[k], z_ss.at[k])
    settle(cnt_x.at[pl.ds(1, NX - 1)], cx_ss)
    for n in range(2):
        settle(cnt_z.at[n, pl.ds(1, 3)], cz_ss.at[n])
    for d in range(1, NY):
        settle(gathered.at[lax.rem(y + NY - d, NY)], y_rs.at[d - 1])
    all_ref[...] = gathered[...]
    for d in range(1, NY):
        y_copy(d).wait_send()


def finish(all_ref, own_ref, upd_hbm, new_hbm, last, sem):
    y = lax.axis_index("tensor")
    keep = pltpu.make_async_copy(own_ref, new_hbm, sem.at[0])
    keep.start()
    iterate = orthogonalize(all_ref[...].reshape(NY * COLS, KVR))
    factor = 0.2 * math.sqrt(max(KVR, NY * COLS))
    last[...] = (factor * iterate.astype(F32)).reshape(NY, COLS, KVR)
    out = pltpu.make_async_copy(last.at[y], upd_hbm, sem.at[1])
    out.start()
    keep.wait()
    out.wait()


def fused(*operands):
    hbm_spec = pl.BlockSpec(memory_space=pltpu.HBM)
    vmem_spec = pl.BlockSpec(memory_space=pltpu.VMEM)
    any_spec = pl.BlockSpec(memory_space=pl.ANY)
    block = jax.ShapeDtypeStruct((COLS, KVR), F32)
    dma = pltpu.SemaphoreType.DMA
    gathered, combined = pl.pallas_call(
        kernel,
        out_shape=(jax.ShapeDtypeStruct((NY, COLS, KVR), BF16), block),
        in_specs=[hbm_spec] * 5,
        out_specs=(vmem_spec, vmem_spec),
        scratch_shapes=[
            pltpu.VMEM((TOK, KVR), BF16),
            pltpu.VMEM((TOK, COLS, MATS), BF16),
            pltpu.SMEM((2, 2), jnp.int32),
            pltpu.VMEM((COLS, KVR), F32),
            pltpu.VMEM((COLS, KVR), F32),
            pltpu.VMEM((2, COLS * PITCH, MATS), F32),
            pltpu.VMEM((KVR, TOK), BF16),
            pltpu.VMEM((COLS // 2, TOK, 2 * MATS), BF16),
            pltpu.VMEM((2, KVR // 128, 8 * PITCH, 128), F32),
            pltpu.VMEM((CHUNKS, 2, NX, NC, NZ, KVR), BF16),
            pltpu.VMEM((CHUNKS, NX, NC, NZ, KVR), BF16),
            pltpu.VMEM((CHUNKS, NX - 1, NC, NZ, KVR), BF16),
            pltpu.VMEM((CHUNKS, NX - 1, NC, NZ, KVR), BF16),
            pltpu.VMEM((KVR // 128, NC * PITCH, 128), F32),
            pltpu.VMEM((CHUNKS, NZ, NC, KVR), BF16),
            pltpu.VMEM((CHUNKS, NZ - 1, NC, KVR), BF16),
            pltpu.VMEM((NY, COLS, KVR), BF16),
            pltpu.VMEM((2, 8, 128), jnp.int32),
            pltpu.VMEM((NX, 8, 128), jnp.int32),
            pltpu.VMEM((2, 4, 8, 128), jnp.int32),
            pltpu.SemaphoreType.REGULAR,
            dma, dma((LOADS,)), dma, dma((2,)),
            dma((CHUNKS,)), dma((CHUNKS,)),
            dma((CHUNKS,)), dma((CHUNKS,)), dma((CHUNKS,)), dma((CHUNKS,)),
            dma, dma((NY - 1,)),
            dma, dma, dma, dma, dma((2,)), dma((2,)),
        ],
        compiler_params=pltpu.CompilerParams(
            collective_id=0, has_side_effects=True, vmem_limit_bytes=48 << 20
        ),
        name="muon_step",
    )(*[pltpu.with_memory_space_constraint(v, pltpu.HBM) for v in operands])
    return pl.pallas_call(
        finish,
        out_shape=(block, block),
        in_specs=[vmem_spec, vmem_spec],
        out_specs=(any_spec, any_spec),
        scratch_shapes=[pltpu.VMEM((NY, COLS, KVR), F32), dma((2,))],
        compiler_params=pltpu.CompilerParams(vmem_limit_bytes=8 << 20),
        name="orthogonal_update",
    )(gathered, combined)


def per_device(latent, out_grad, lengths, momentum, accumulated):
    update, combined = fused(
        latent,
        out_grad,
        lengths,
        jnp.swapaxes(momentum[0], 0, 1),
        jnp.swapaxes(accumulated[0], 0, 1),
    )
    return (jnp.swapaxes(update, 0, 1)[None], jnp.swapaxes(combined, 0, 1)[None])


def solution(mesh):
    owned = P(("dp", "expert"), None, "tensor")
    in_specs = (
        P(("dp", "expert"), None),
        P(("dp", "expert"), "tensor", None),
        P(None, ("dp", "expert")),
        owned,
        owned,
    )
    return jax.shard_map(
        per_device, mesh=mesh, in_specs=in_specs, out_specs=(owned, owned), check_vma=False
    )
```

```python
import functools
import math

import jax
import jax.numpy as jnp
from jax import lax
from jax.experimental import pallas as pl
from jax.experimental.pallas import tpu as pltpu
from jax.sharding import PartitionSpec as P

ITERS = 5
EPSILON = 1e-07
COEFF_A = 3.4445
COEFF_B = -4.775
COEFF_C = 2.0315
DECAY = 0.95

TOK = 1024
KVR = 384
COLS = 16
MATS = 128
NX = 4
NY = 4
NZ = 16
SEQ = 512
CHUNKS = 4
NC = COLS // CHUNKS
LOADS = 2
PITCH = 17
F32 = jnp.float32
BF16 = jnp.bfloat16
MESH = pl.DeviceIdType.MESH


def device(core, x, y, z):
    return (lax.rem(z, 8) * 2 + core, y, x * 2 + z // 8)


def orthogonalize(iterate):
    wide = iterate.astype(F32)
    scale = 1.0 / (jnp.sqrt(jnp.sum(wide * wide, axis=(0, 1), keepdims=True)) + EPSILON)
    for step in range(ITERS):
        gram = lax.dot_general(
            iterate, iterate, (((1,), (1,)), ((), ())), preferred_element_type=F32
        )
        if step == 0:
            gram = gram * scale * scale
        high = gram.astype(BF16)
        low = (gram - high.astype(F32)).astype(BF16)
        squared = (
            jnp.dot(high, high, preferred_element_type=F32)
            + jnp.dot(high, low, preferred_element_type=F32)
            + jnp.dot(low, high, preferred_element_type=F32)
        )
        poly = (COEFF_B * gram + COEFF_C * squared).astype(BF16)
        moved = COEFF_A * iterate.astype(F32) + jnp.dot(poly, iterate, preferred_element_type=F32)
        if step == 0:
            moved = moved * scale
        iterate = moved.astype(BF16)
    return iterate


def kernel(
    lat_hbm, og_hbm, len_hbm, mom_hbm, acc_hbm, all_ref, new_ref,
    lat, og, lens, mom, acc, flat, lat_t, right, turned,
    send_a, recv_a, send_x, recv_x, part, send_z, recv_z, gathered,
    cnt_a, cnt_x, cnt_z,
    known, lat_sem, og_sem, len_sem, mom_sem,
    a_ss, a_rs, x_ss, x_rs, z_ss, z_rs, y_ss, y_rs,
    ca_ss, ca_rs, cx_ss, cx_rs, cz_ss, cz_rs,
):
    dp = lax.axis_index("dp")
    y = lax.axis_index("tensor")
    expert = lax.axis_index("expert")
    core = lax.rem(dp, 2)
    x = expert // 2
    z = lax.rem(expert, 2) * 8 + dp // 2

    sibling = device(1 - core, x, y, z)
    x_peers = [device(core, lax.rem(x + d, NX), y, z) for d in range(1, NX)]
    y_peers = [device(core, x, lax.rem(y + d, NY), z) for d in range(1, NY)]
    z_order = sorted(range(1, NZ), key=lambda d: -min(d, NZ - d))
    z_peers = {d: device(core, x, y, lax.rem(z + d, NZ)) for d in z_order}

    step = TOK // LOADS
    len_copy = pltpu.make_async_copy(len_hbm, lens, len_sem)
    len_copy.start()
    lat_copy = pltpu.make_async_copy(lat_hbm, lat, lat_sem)
    lat_copy.start()
    og_copies = []
    for i in range(LOADS):
        cut = pl.ds(i * step, step)
        copy = pltpu.make_async_copy(og_hbm.at[cut], og.at[cut], og_sem.at[i])
        copy.start()
        og_copies.append(copy)
    barrier = pltpu.get_barrier_semaphore()
    near = [z_peers[d] for d in (4, NZ - 4, 3, NZ - 3)]
    near += [x_peers[1], y_peers[1], z_peers[2], z_peers[NZ - 2], x_peers[0], x_peers[2]]
    near += [y_peers[0], y_peers[2], z_peers[1], z_peers[NZ - 1], sibling]
    for peer in near:
        pl.semaphore_signal(barrier, inc=1, device_id=peer, device_id_type=MESH)

    mom_copies = [
        pltpu.make_async_copy(mom_hbm, mom, mom_sem.at[0]),
        pltpu.make_async_copy(acc_hbm, acc, mom_sem.at[1]),
    ]
    for copy in mom_copies:
        copy.start()

    len_copy.wait()
    own = lens[0, 0] + lens[0, 1] + lens[1, 0] + lens[1, 1]
    cnt_a[0] = jnp.full((8, 128), own, jnp.int32)

    lat_copy.wait()
    token = lax.broadcasted_iota(jnp.int32, (TOK, 1), 0)
    limit = jnp.where(token < SEQ, lens[1, 0], lens[1, 1] + SEQ)
    masked = jnp.where(token < limit, lat[...].astype(F32), 0.0)
    lat_t[...] = masked.T.astype(BF16)

    for i in range(LOADS):
        og_copies[i].wait()

        def regroup(j, _):
            base = pl.multiple_of(i * step + j * 32, 32)
            for h in range(2):
                rows = og[pl.ds(base + h * 16, 16)].astype(F32)
                for t in range(16):
                    flat[h, pl.ds(t, COLS, stride=PITCH), :] = rows[t]
                for c in range(COLS):
                    picked = flat[h, pl.ds(c * PITCH, 16), :]
                    right[c // 2, pl.ds(base + h * 16, 16), (c % 2) * MATS : (c % 2 + 1) * MATS] = (
                        picked.astype(BF16)
                    )
            return 0

        lax.fori_loop(0, step // 32, regroup, 0)

    def multiply(k):
        for p in range(k * NC // 2, (k + 1) * NC // 2):
            product = jnp.dot(lat_t[...], right[p], preferred_element_type=F32)
            for h in range(2):
                c = p * 2 + h
                for b in range(KVR // 128):
                    lanes = slice(b * 128, (b + 1) * 128)
                    block = product[lanes, h * MATS : (h + 1) * MATS].T
                    for t in range(8):
                        turned[h, b, pl.ds(t * PITCH, 16), :] = block[t * 16 : (t + 1) * 16]
                    for cc in range(2):
                        for xx in range(NX):
                            q = cc * 8 + xx * 2
                            low = turned[h, b, pl.ds(q, 8, stride=PITCH), :]
                            high = turned[h, b, pl.ds(q + 1, 8, stride=PITCH), :]
                            send_a[k, cc, xx, c - k * NC, :, lanes] = jnp.concatenate(
                                [low, high], 0
                            ).astype(BF16)

    pl.semaphore_wait(barrier, len(near))
    for d in (4, NZ - 4):
        pl.semaphore_signal(known, inc=1, device_id=z_peers[d], device_id_type=MESH)
    multiply(0)

    def count_copy(src, dst, ss, rs, peer):
        return pltpu.make_async_remote_copy(src, dst, ss, rs, device_id=peer, device_id_type=MESH)

    ca = count_copy(cnt_a.at[0], cnt_a.at[1], ca_ss, ca_rs, sibling)

    def core_copy(k):
        return pltpu.make_async_remote_copy(
            send_a.at[k, 1 - core], recv_a.at[k], a_ss.at[k], a_rs.at[k],
            device_id=sibling, device_id_type=MESH,
        )

    def pair_sum(k, xx):
        return send_a[k, core, xx].astype(F32) + recv_a[k, xx].astype(F32)

    def x_copy(k, d):
        return pltpu.make_async_remote_copy(
            send_x.at[k, d - 1], recv_x.at[k, d - 1], x_ss.at[k], x_rs.at[k],
            device_id=x_peers[d - 1], device_id_type=MESH,
        )

    def z_copy(k, d):
        return pltpu.make_async_remote_copy(
            send_z.at[k, lax.rem(z + d, NZ)], recv_z.at[k, d - 1], z_ss.at[k], z_rs.at[k],
            device_id=z_peers[d], device_id_type=MESH,
        )

    def settle(ref, sem):
        pltpu.make_async_copy(ref, ref, sem).wait()

    cx = [
        count_copy(cnt_x.at[0], cnt_x.at[d], cx_ss, cx_rs, x_peers[d - 1]) for d in range(1, NX)
    ]
    cz = [
        count_copy(cnt_z.at[0, 0], cnt_z.at[0, 1 + n], cz_ss.at[0], cz_rs.at[0], z_peers[d])
        for n, d in enumerate((1, NZ - 1, 2))
    ]
    cw = [
        count_copy(cnt_z.at[1, 0], cnt_z.at[1, 1 + n], cz_ss.at[1], cz_rs.at[1], z_peers[d])
        for n, d in enumerate((4, NZ - 4, 8))
    ]

    def total_of(ref, sem):
        settle(ref.at[pl.ds(1, 3)], sem)
        return ref[0] + ref[1] + ref[2] + ref[3]

    def start_count(k):
        if k == 0:
            cnt_z[0, 0] = total_of(cnt_x, cx_rs)
            for copy in cz:
                copy.start()
        if k == 1:
            cnt_z[1, 0] = total_of(cnt_z.at[0], cz_rs.at[0])
            for copy in cw:
                copy.start()

    def start_x(k):
        core_copy(k).wait_recv()
        for d in (2, 1, 3):
            send_x[k, d - 1] = pair_sum(k, lax.rem(x + d, NX)).astype(BF16)
            x_copy(k, d).start()
        if k == 0:
            ca.wait_recv()
            cnt_x[0] = cnt_a[0] + cnt_a[1]
            for copy in cx:
                copy.start()

    def start_z(k):
        total = pair_sum(k, x)
        settle(recv_x.at[k], x_rs.at[k])
        for d in (1, 3, 2):
            total = total + recv_x[k, d - 1].astype(F32)
        for b in range(KVR // 128):
            for c in range(NC):
                part[b, pl.ds(c * PITCH, NZ), :] = total[c, :, b * 128 : (b + 1) * 128]
        for d in z_order + [0]:
            t = lax.rem(z + d, NZ)
            for b in range(KVR // 128):
                send_z[k, t, :, b * 128 : (b + 1) * 128] = part[b, pl.ds(t, NC, stride=PITCH), :].astype(BF16)
            if d:
                z_copy(k, d).start()

    for k in range(CHUNKS):
        if k >= 1:
            multiply(k)
        core_copy(k).start()
        if k == 0:
            ca.start()
        if k >= 1:
            start_x(k - 1)
    start_x(CHUNKS - 1)
    pl.semaphore_wait(known, 2)
    for k in range(CHUNKS):
        start_z(k)
        start_count(k)

    for copy in mom_copies:
        copy.wait()
    count = total_of(cnt_z.at[1], cz_rs.at[1])
    scale = 1.0 / count[0:1, 0:1].astype(F32)

    for k in range(CHUNKS):
        grad = send_z[k, z].astype(F32)
        settle(recv_z.at[k], z_rs.at[k])
        for d in z_order:
            grad = grad + recv_z[k, d - 1].astype(F32)
        own = pl.ds(k * NC, NC)
        new_ref[own] = DECAY * mom[own] + acc[own] + grad * scale
    gathered[y] = new_ref[...].astype(BF16)

    def y_copy(d):
        return pltpu.make_async_remote_copy(
            gathered.at[y], gathered.at[y], y_ss, y_rs.at[d - 1],
            device_id=y_peers[d - 1], device_id_type=MESH,
        )

    for d in (2, 1, 3):
        y_copy(d).start()
    ca.wait_send()
    for k in range(CHUNKS):
        core_copy(k).wait_send()
        settle(recv_x.at[k], x_ss.at[k])
        settle(recv_z.at[k], z_ss.at[k])
    settle(cnt_x.at[pl.ds(1, NX - 1)], cx_ss)
    for n in range(2):
        settle(cnt_z.at[n, pl.ds(1, 3)], cz_ss.at[n])
    for d in range(1, NY):
        settle(gathered.at[lax.rem(y + NY - d, NY)], y_rs.at[d - 1])
    all_ref[...] = gathered[...]
    for d in range(1, NY):
        y_copy(d).wait_send()


def finish(all_ref, own_ref, upd_hbm, new_hbm, last, sem):
    y = lax.axis_index("tensor")
    keep = pltpu.make_async_copy(own_ref, new_hbm, sem.at[0])
    keep.start()
    iterate = orthogonalize(all_ref[...].reshape(NY * COLS, KVR))
    factor = 0.2 * math.sqrt(max(KVR, NY * COLS))
    last[...] = (factor * iterate.astype(F32)).reshape(NY, COLS, KVR)
    out = pltpu.make_async_copy(last.at[y], upd_hbm, sem.at[1])
    out.start()
    keep.wait()
    out.wait()


def fused(*operands):
    hbm_spec = pl.BlockSpec(memory_space=pltpu.HBM)
    vmem_spec = pl.BlockSpec(memory_space=pltpu.VMEM)
    any_spec = pl.BlockSpec(memory_space=pl.ANY)
    block = jax.ShapeDtypeStruct((COLS, KVR), F32)
    dma = pltpu.SemaphoreType.DMA
    gathered, combined = pl.pallas_call(
        kernel,
        out_shape=(jax.ShapeDtypeStruct((NY, COLS, KVR), BF16), block),
        in_specs=[hbm_spec] * 5,
        out_specs=(vmem_spec, vmem_spec),
        scratch_shapes=[
            pltpu.VMEM((TOK, KVR), BF16),
            pltpu.VMEM((TOK, COLS, MATS), BF16),
            pltpu.SMEM((2, 2), jnp.int32),
            pltpu.VMEM((COLS, KVR), F32),
            pltpu.VMEM((COLS, KVR), F32),
            pltpu.VMEM((2, COLS * PITCH, MATS), F32),
            pltpu.VMEM((KVR, TOK), BF16),
            pltpu.VMEM((COLS // 2, TOK, 2 * MATS), BF16),
            pltpu.VMEM((2, KVR // 128, 8 * PITCH, 128), F32),
            pltpu.VMEM((CHUNKS, 2, NX, NC, NZ, KVR), BF16),
            pltpu.VMEM((CHUNKS, NX, NC, NZ, KVR), BF16),
            pltpu.VMEM((CHUNKS, NX - 1, NC, NZ, KVR), BF16),
            pltpu.VMEM((CHUNKS, NX - 1, NC, NZ, KVR), BF16),
            pltpu.VMEM((KVR // 128, NC * PITCH, 128), F32),
            pltpu.VMEM((CHUNKS, NZ, NC, KVR), BF16),
            pltpu.VMEM((CHUNKS, NZ - 1, NC, KVR), BF16),
            pltpu.VMEM((NY, COLS, KVR), BF16),
            pltpu.VMEM((2, 8, 128), jnp.int32),
            pltpu.VMEM((NX, 8, 128), jnp.int32),
            pltpu.VMEM((2, 4, 8, 128), jnp.int32),
            pltpu.SemaphoreType.REGULAR,
            dma, dma((LOADS,)), dma, dma((2,)),
            dma((CHUNKS,)), dma((CHUNKS,)),
            dma((CHUNKS,)), dma((CHUNKS,)), dma((CHUNKS,)), dma((CHUNKS,)),
            dma, dma((NY - 1,)),
            dma, dma, dma, dma, dma((2,)), dma((2,)),
        ],
        compiler_params=pltpu.CompilerParams(
            collective_id=0, has_side_effects=True, vmem_limit_bytes=48 << 20
        ),
        name="muon_step",
    )(*[pltpu.with_memory_space_constraint(v, pltpu.HBM) for v in operands])
    return pl.pallas_call(
        finish,
        out_shape=(block, block),
        in_specs=[vmem_spec, vmem_spec],
        out_specs=(any_spec, any_spec),
        scratch_shapes=[pltpu.VMEM((NY, COLS, KVR), F32), dma((2,))],
        compiler_params=pltpu.CompilerParams(vmem_limit_bytes=8 << 20),
        name="orthogonal_update",
    )(gathered, combined)


def per_device(latent, out_grad, lengths, momentum, accumulated):
    update, combined = fused(
        latent,
        out_grad,
        lengths,
        jnp.swapaxes(momentum[0], 0, 1),
        jnp.swapaxes(accumulated[0], 0, 1),
    )
    return (jnp.swapaxes(update, 0, 1)[None], jnp.swapaxes(combined, 0, 1)[None])


def solution(mesh):
    owned = P(("dp", "expert"), None, "tensor")
    in_specs = (
        P(("dp", "expert"), None),
        P(("dp", "expert"), "tensor", None),
        P(None, ("dp", "expert")),
        owned,
        owned,
    )
    return jax.shard_map(
        per_device, mesh=mesh, in_specs=in_specs, out_specs=(owned, owned), check_vma=False
    )
```

```python
import functools
import math

import jax
import jax.numpy as jnp
from jax import lax
from jax.experimental import pallas as pl
from jax.experimental.pallas import tpu as pltpu
from jax.sharding import PartitionSpec as P

ITERS = 5
EPSILON = 1e-07
COEFF_A = 3.4445
COEFF_B = -4.775
COEFF_C = 2.0315
DECAY = 0.95

TOK = 1024
KVR = 384
COLS = 16
MATS = 128
NX = 4
NY = 4
NZ = 16
SEQ = 512
CHUNKS = 4
NC = COLS // CHUNKS
LOADS = 1
PITCH = 17
F32 = jnp.float32
BF16 = jnp.bfloat16
MESH = pl.DeviceIdType.MESH


def device(core, x, y, z):
    return (lax.rem(z, 8) * 2 + core, y, x * 2 + z // 8)


def orthogonalize(iterate):
    wide = iterate.astype(F32)
    scale = 1.0 / (jnp.sqrt(jnp.sum(wide * wide, axis=(0, 1), keepdims=True)) + EPSILON)
    for step in range(ITERS):
        gram = lax.dot_general(
            iterate, iterate, (((1,), (1,)), ((), ())), preferred_element_type=F32
        )
        if step == 0:
            gram = gram * scale * scale
        high = gram.astype(BF16)
        low = (gram - high.astype(F32)).astype(BF16)
        squared = (
            jnp.dot(high, high, preferred_element_type=F32)
            + jnp.dot(high, low, preferred_element_type=F32)
            + jnp.dot(low, high, preferred_element_type=F32)
        )
        poly = (COEFF_B * gram + COEFF_C * squared).astype(BF16)
        moved = COEFF_A * iterate.astype(F32) + jnp.dot(poly, iterate, preferred_element_type=F32)
        if step == 0:
            moved = moved * scale
        iterate = moved.astype(BF16)
    return iterate


def kernel(
    lat_hbm, og_hbm, len_hbm, mom_hbm, acc_hbm, all_ref, new_ref,
    lat, og, lens, mom, acc, flat, lat_t, right, turned,
    send_a, recv_a, send_x, recv_x, part, send_z, recv_z, gathered,
    cnt_a, cnt_x, cnt_z,
    known, lat_sem, og_sem, len_sem, mom_sem,
    a_ss, a_rs, x_ss, x_rs, z_ss, z_rs, y_ss, y_rs,
    ca_ss, ca_rs, cx_ss, cx_rs, cz_ss, cz_rs,
):
    dp = lax.axis_index("dp")
    y = lax.axis_index("tensor")
    expert = lax.axis_index("expert")
    core = lax.rem(dp, 2)
    x = expert // 2
    z = lax.rem(expert, 2) * 8 + dp // 2

    sibling = device(1 - core, x, y, z)
    x_peers = [device(core, lax.rem(x + d, NX), y, z) for d in range(1, NX)]
    y_peers = [device(core, x, lax.rem(y + d, NY), z) for d in range(1, NY)]
    z_order = sorted(range(1, NZ), key=lambda d: -min(d, NZ - d))
    z_peers = {d: device(core, x, y, lax.rem(z + d, NZ)) for d in z_order}

    step = TOK // LOADS
    len_copy = pltpu.make_async_copy(len_hbm, lens, len_sem)
    len_copy.start()
    lat_copy = pltpu.make_async_copy(lat_hbm, lat, lat_sem)
    lat_copy.start()
    og_copies = []
    for i in range(LOADS):
        cut = pl.ds(i * step, step)
        copy = pltpu.make_async_copy(og_hbm.at[cut], og.at[cut], og_sem.at[i])
        copy.start()
        og_copies.append(copy)
    barrier = pltpu.get_barrier_semaphore()
    near = [z_peers[d] for d in (4, NZ - 4, 3, NZ - 3)]
    near += [x_peers[1], y_peers[1], z_peers[2], z_peers[NZ - 2], x_peers[0], x_peers[2]]
    near += [y_peers[0], y_peers[2], z_peers[1], z_peers[NZ - 1], sibling]
    for peer in near:
        pl.semaphore_signal(barrier, inc=1, device_id=peer, device_id_type=MESH)

    mom_copies = [
        pltpu.make_async_copy(mom_hbm, mom, mom_sem.at[0]),
        pltpu.make_async_copy(acc_hbm, acc, mom_sem.at[1]),
    ]
    for copy in mom_copies:
        copy.start()

    len_copy.wait()
    own = lens[0, 0] + lens[0, 1] + lens[1, 0] + lens[1, 1]
    cnt_a[0] = jnp.full((8, 128), own, jnp.int32)

    lat_copy.wait()
    token = lax.broadcasted_iota(jnp.int32, (TOK, 1), 0)
    limit = jnp.where(token < SEQ, lens[1, 0], lens[1, 1] + SEQ)
    masked = jnp.where(token < limit, lat[...].astype(F32), 0.0)
    lat_t[...] = masked.T.astype(BF16)

    for i in range(LOADS):
        og_copies[i].wait()

        def regroup(j, _):
            base = pl.multiple_of(i * step + j * 32, 32)
            for h in range(2):
                rows = og[pl.ds(base + h * 16, 16)].astype(F32)
                for t in range(16):
                    flat[h, pl.ds(t, COLS, stride=PITCH), :] = rows[t]
                for c in range(COLS):
                    picked = flat[h, pl.ds(c * PITCH, 16), :]
                    right[c // 2, pl.ds(base + h * 16, 16), (c % 2) * MATS : (c % 2 + 1) * MATS] = (
                        picked.astype(BF16)
                    )
            return 0

        lax.fori_loop(0, step // 32, regroup, 0)

    def multiply(k):
        for p in range(k * NC // 2, (k + 1) * NC // 2):
            product = jnp.dot(lat_t[...], right[p], preferred_element_type=F32)
            for h in range(2):
                c = p * 2 + h
                for b in range(KVR // 128):
                    lanes = slice(b * 128, (b + 1) * 128)
                    block = product[lanes, h * MATS : (h + 1) * MATS].T
                    for t in range(8):
                        turned[h, b, pl.ds(t * PITCH, 16), :] = block[t * 16 : (t + 1) * 16]
                    for cc in range(2):
                        for xx in range(NX):
                            q = cc * 8 + xx * 2
                            low = turned[h, b, pl.ds(q, 8, stride=PITCH), :]
                            high = turned[h, b, pl.ds(q + 1, 8, stride=PITCH), :]
                            send_a[k, cc, xx, c - k * NC, :, lanes] = jnp.concatenate(
                                [low, high], 0
                            ).astype(BF16)

    pl.semaphore_wait(barrier, len(near))
    for d in (4, NZ - 4):
        pl.semaphore_signal(known, inc=1, device_id=z_peers[d], device_id_type=MESH)
    multiply(0)

    def count_copy(src, dst, ss, rs, peer):
        return pltpu.make_async_remote_copy(src, dst, ss, rs, device_id=peer, device_id_type=MESH)

    ca = count_copy(cnt_a.at[0], cnt_a.at[1], ca_ss, ca_rs, sibling)

    def core_copy(k):
        return pltpu.make_async_remote_copy(
            send_a.at[k, 1 - core], recv_a.at[k], a_ss.at[k], a_rs.at[k],
            device_id=sibling, device_id_type=MESH,
        )

    def pair_sum(k, xx):
        return send_a[k, core, xx].astype(F32) + recv_a[k, xx].astype(F32)

    def x_copy(k, d):
        return pltpu.make_async_remote_copy(
            send_x.at[k, d - 1], recv_x.at[k, d - 1], x_ss.at[k], x_rs.at[k],
            device_id=x_peers[d - 1], device_id_type=MESH,
        )

    def z_copy(k, d):
        return pltpu.make_async_remote_copy(
            send_z.at[k, lax.rem(z + d, NZ)], recv_z.at[k, d - 1], z_ss.at[k], z_rs.at[k],
            device_id=z_peers[d], device_id_type=MESH,
        )

    def settle(ref, sem):
        pltpu.make_async_copy(ref, ref, sem).wait()

    cx = [
        count_copy(cnt_x.at[0], cnt_x.at[d], cx_ss, cx_rs, x_peers[d - 1]) for d in range(1, NX)
    ]
    cz = [
        count_copy(cnt_z.at[0, 0], cnt_z.at[0, 1 + n], cz_ss.at[0], cz_rs.at[0], z_peers[d])
        for n, d in enumerate((1, NZ - 1, 2))
    ]
    cw = [
        count_copy(cnt_z.at[1, 0], cnt_z.at[1, 1 + n], cz_ss.at[1], cz_rs.at[1], z_peers[d])
        for n, d in enumerate((4, NZ - 4, 8))
    ]

    def total_of(ref, sem):
        settle(ref.at[pl.ds(1, 3)], sem)
        return ref[0] + ref[1] + ref[2] + ref[3]

    def start_count(k):
        if k == 0:
            cnt_z[0, 0] = total_of(cnt_x, cx_rs)
            for copy in cz:
                copy.start()
        if k == 1:
            cnt_z[1, 0] = total_of(cnt_z.at[0], cz_rs.at[0])
            for copy in cw:
                copy.start()

    def start_x(k):
        core_copy(k).wait_recv()
        for d in (2, 1, 3):
            send_x[k, d - 1] = pair_sum(k, lax.rem(x + d, NX)).astype(BF16)
            x_copy(k, d).start()
        if k == 0:
            ca.wait_recv()
            cnt_x[0] = cnt_a[0] + cnt_a[1]
            for copy in cx:
                copy.start()

    def start_z(k):
        total = pair_sum(k, x)
        settle(recv_x.at[k], x_rs.at[k])
        for d in (1, 3, 2):
            total = total + recv_x[k, d - 1].astype(F32)
        for b in range(KVR // 128):
            for c in range(NC):
                part[b, pl.ds(c * PITCH, NZ), :] = total[c, :, b * 128 : (b + 1) * 128]
        for d in z_order + [0]:
            t = lax.rem(z + d, NZ)
            for b in range(KVR // 128):
                send_z[k, t, :, b * 128 : (b + 1) * 128] = part[b, pl.ds(t, NC, stride=PITCH), :].astype(BF16)
            if d:
                z_copy(k, d).start()

    for k in range(CHUNKS):
        if k >= 1:
            multiply(k)
        core_copy(k).start()
        if k == 0:
            ca.start()
        if k >= 1:
            start_x(k - 1)
    start_x(CHUNKS - 1)
    pl.semaphore_wait(known, 2)
    for k in range(CHUNKS):
        start_z(k)
        start_count(k)

    for copy in mom_copies:
        copy.wait()
    count = total_of(cnt_z.at[1], cz_rs.at[1])
    scale = 1.0 / count[0:1, 0:1].astype(F32)

    for k in range(CHUNKS):
        grad = send_z[k, z].astype(F32)
        settle(recv_z.at[k], z_rs.at[k])
        for d in z_order:
            grad = grad + recv_z[k, d - 1].astype(F32)
        own = pl.ds(k * NC, NC)
        new_ref[own] = DECAY * mom[own] + acc[own] + grad * scale
    gathered[y] = new_ref[...].astype(BF16)

    def y_copy(d):
        return pltpu.make_async_remote_copy(
            gathered.at[y], gathered.at[y], y_ss, y_rs.at[d - 1],
            device_id=y_peers[d - 1], device_id_type=MESH,
        )

    for d in (2, 1, 3):
        y_copy(d).start()
    ca.wait_send()
    for k in range(CHUNKS):
        core_copy(k).wait_send()
        settle(recv_x.at[k], x_ss.at[k])
        settle(recv_z.at[k], z_ss.at[k])
    settle(cnt_x.at[pl.ds(1, NX - 1)], cx_ss)
    for n in range(2):
        settle(cnt_z.at[n, pl.ds(1, 3)], cz_ss.at[n])
    for d in range(1, NY):
        settle(gathered.at[lax.rem(y + NY - d, NY)], y_rs.at[d - 1])
    all_ref[...] = gathered[...]
    for d in range(1, NY):
        y_copy(d).wait_send()


def finish(all_ref, own_ref, upd_hbm, new_hbm, last, sem):
    y = lax.axis_index("tensor")
    keep = pltpu.make_async_copy(own_ref, new_hbm, sem.at[0])
    keep.start()
    iterate = orthogonalize(all_ref[...].reshape(NY * COLS, KVR))
    factor = 0.2 * math.sqrt(max(KVR, NY * COLS))
    last[...] = (factor * iterate.astype(F32)).reshape(NY, COLS, KVR)
    out = pltpu.make_async_copy(last.at[y], upd_hbm, sem.at[1])
    out.start()
    keep.wait()
    out.wait()


def fused(*operands):
    hbm_spec = pl.BlockSpec(memory_space=pltpu.HBM)
    vmem_spec = pl.BlockSpec(memory_space=pltpu.VMEM)
    any_spec = pl.BlockSpec(memory_space=pl.ANY)
    block = jax.ShapeDtypeStruct((COLS, KVR), F32)
    dma = pltpu.SemaphoreType.DMA
    gathered, combined = pl.pallas_call(
        kernel,
        out_shape=(jax.ShapeDtypeStruct((NY, COLS, KVR), BF16), block),
        in_specs=[hbm_spec] * 5,
        out_specs=(vmem_spec, vmem_spec),
        scratch_shapes=[
            pltpu.VMEM((TOK, KVR), BF16),
            pltpu.VMEM((TOK, COLS, MATS), BF16),
            pltpu.SMEM((2, 2), jnp.int32),
            pltpu.VMEM((COLS, KVR), F32),
            pltpu.VMEM((COLS, KVR), F32),
            pltpu.VMEM((2, COLS * PITCH, MATS), F32),
            pltpu.VMEM((KVR, TOK), BF16),
            pltpu.VMEM((COLS // 2, TOK, 2 * MATS), BF16),
            pltpu.VMEM((2, KVR // 128, 8 * PITCH, 128), F32),
            pltpu.VMEM((CHUNKS, 2, NX, NC, NZ, KVR), BF16),
            pltpu.VMEM((CHUNKS, NX, NC, NZ, KVR), BF16),
            pltpu.VMEM((CHUNKS, NX - 1, NC, NZ, KVR), BF16),
            pltpu.VMEM((CHUNKS, NX - 1, NC, NZ, KVR), BF16),
            pltpu.VMEM((KVR // 128, NC * PITCH, 128), F32),
            pltpu.VMEM((CHUNKS, NZ, NC, KVR), BF16),
            pltpu.VMEM((CHUNKS, NZ - 1, NC, KVR), BF16),
            pltpu.VMEM((NY, COLS, KVR), BF16),
            pltpu.VMEM((2, 8, 128), jnp.int32),
            pltpu.VMEM((NX, 8, 128), jnp.int32),
            pltpu.VMEM((2, 4, 8, 128), jnp.int32),
            pltpu.SemaphoreType.REGULAR,
            dma, dma((LOADS,)), dma, dma((2,)),
            dma((CHUNKS,)), dma((CHUNKS,)),
            dma((CHUNKS,)), dma((CHUNKS,)), dma((CHUNKS,)), dma((CHUNKS,)),
            dma, dma((NY - 1,)),
            dma, dma, dma, dma, dma((2,)), dma((2,)),
        ],
        compiler_params=pltpu.CompilerParams(
            collective_id=0, has_side_effects=True, vmem_limit_bytes=48 << 20
        ),
        name="muon_step",
    )(*[pltpu.with_memory_space_constraint(v, pltpu.HBM) for v in operands])
    return pl.pallas_call(
        finish,
        out_shape=(block, block),
        in_specs=[vmem_spec, vmem_spec],
        out_specs=(any_spec, any_spec),
        scratch_shapes=[pltpu.VMEM((NY, COLS, KVR), F32), dma((2,))],
        compiler_params=pltpu.CompilerParams(vmem_limit_bytes=8 << 20),
        name="orthogonal_update",
    )(gathered, combined)


def per_device(latent, out_grad, lengths, momentum, accumulated):
    update, combined = fused(
        latent,
        out_grad,
        lengths,
        jnp.swapaxes(momentum[0], 0, 1),
        jnp.swapaxes(accumulated[0], 0, 1),
    )
    return (jnp.swapaxes(update, 0, 1)[None], jnp.swapaxes(combined, 0, 1)[None])


def solution(mesh):
    owned = P(("dp", "expert"), None, "tensor")
    in_specs = (
        P(("dp", "expert"), None),
        P(("dp", "expert"), "tensor", None),
        P(None, ("dp", "expert")),
        owned,
        owned,
    )
    return jax.shard_map(
        per_device, mesh=mesh, in_specs=in_specs, out_specs=(owned, owned), check_vma=False
    )
```
